32 devices in a mesh: groups: 1, cache: 16 (over z, y, x), dp: 2 (over core).
Axes of the slice: x: 2, y: 2, z: 4, core: 2. Of those that a mesh axis runs over, the one named last changes fastest.
Arguments:
- hidden: bfloat16 [640, 8192], P(('groups', 'dp'), 'cache'), may hold values from -6 to 6
- out_grad: bfloat16 [640, 8192], P(('groups', 'dp'), 'cache'), may hold values from -192 to 192
- norm_gain: float32 [8192], replicated, may hold values from 0.25 to 1.75
- w_query: bfloat16 [8192, 2048], P(None, 'cache'), may hold values from -0.0625 to 0.0625
- w_key: bfloat16 [8192, 8, 128], P(None, None, 'cache'), may hold values from -0.1875 to 0.1875
- w_value: bfloat16 [8192, 8, 128], P(None, None, 'cache'), may hold values from -0.0625 to 0.0625
- w_out: bfloat16 [2048, 8192], P('cache'), may hold values from -0.125 to 0.125
- cache_keys: float32 [1024, 1024], P(('groups', 'cache', 'dp')), may hold values from -512 to 512
- cache_values: float32 [1024, 1024], P(('groups', 'cache', 'dp')), may hold values from -6 to 6
- first_moment: float32 [2, 1024, 1024], P(None, ('groups', 'cache', 'dp')), may hold values from -0.1875 to 0.1875
- second_moment: float32 [2, 1024, 1024], P(None, ('groups', 'cache', 'dp')), may hold values from 0.0001 to 0.002
- conv_lengths: int32 [2, 4], P(('groups', 'dp')), may hold values from 1 to 160, 320 in all within a row
- row_offsets: int32 [2, 4], P(('groups', 'dp')), may hold values from 0 to 1023
Outputs:
- new_keys: float32 [1024, 1024], P(('groups', 'cache', 'dp'))
- new_values: float32 [1024, 1024], P(('groups', 'cache', 'dp'))
- new_first: float32 [2, 1024, 1024], P(None, ('groups', 'cache', 'dp'))
- new_second: float32 [2, 1024, 1024], P(None, ('groups', 'cache', 'dp'))
The draws below stay inside these ranges and needn't reach their ends.
Inputs may be any that keep to these rules, and one draw needn't show every extreme that they name: `conv_lengths`: each dp index's 4 lengths sum to 320, and one of them is 160.
All inputs are finite; a program needn't handle non-finite values.
Results may differ from the reference program's by a relative error of at most 0.006.
The reference program's roundings to bfloat16 on the way count: a program that leaves them out, or rounds other values in their place, can miss the bound.
Values may be sent and summed in bfloat16 or wider, within the bound.
A program may use at most 128 MiB of HBM per device.

```python
import math
import jax
import jax.numpy as jnp
import numpy as np
from jax import lax

D = 8192
HEAD = 128
KV = 8
HEADS = 16
CACHE_LEN = 1024
TOK_DEV = 320
TOKENS = 640
CONV = 4
CONV_MOST = 160
OFFSET_MAX = 1024
ADAM_STEP = 10
N_DP = 2


def draw_cache_keys(key, part):
    baseline = jax.random.truncated_normal(jax.random.fold_in(key, 11), -6.0, 6.0, (CACHE_LEN, KV * HEAD), jnp.float32)
    return baseline


def touch_ends(drawn, stream_key, least, largest):
    longest = drawn.shape.index(max(drawn.shape))
    spots = []
    for shift in (0, 1):
        where = [jax.random.randint(jax.random.fold_in(stream_key, axis), (), 0, length) for axis, length in enumerate(drawn.shape)]
        where[longest] = (where[longest] + shift) % drawn.shape[longest]
        spots.append(tuple(where))
    return drawn.at[spots[0]].set(least).at[spots[1]].set(largest)


def level_of(rng, shape, cuts, low, high):
    factor_of = 1.0
    for dim, blocks in cuts:
        draws = jax.random.uniform(jax.random.fold_in(jax.random.fold_in(rng, 6), dim), (blocks,), jnp.float32, low / len(cuts), high / len(cuts))
        factor_of = factor_of * jnp.repeat(jnp.exp(draws), shape[dim] // blocks).reshape((-1,) + (1,) * (len(shape) - 1 - dim))
    return factor_of


def split_up(amount, total, limit, skew):
    weights = [(1 << 20) // math.isqrt(rank ** skew) + 1 for rank in range(2, amount + 1)]
    rest, counts = total - limit - (amount - 1), [1] * (amount - 1)
    while rest > 0:
        free = [i for i in range(amount - 1) if counts[i] < limit]
        mass, left = sum([weights[i] for i in free]), rest
        for i in free:
            addition = min(limit - counts[i], max(1, left * weights[i] // mass), rest)
            counts[i] = counts[i] + addition
            rest = rest - addition
    return np.array([limit] + counts)


def ragged(own_key, amount, total, most, lean):
    if amount == 2:
        one = jax.random.randint(own_key, (), max(1, total - most), min(most, total - 1) + 1)
        return jnp.stack([one, total - one])
    sizes = jnp.asarray(split_up(amount, total, most, lean), jnp.int32)
    couples = (amount - 1) // 2
    donor, sink = sizes[1:1 + 2 * couples:2], sizes[2:2 + 2 * couples:2]
    room = jnp.minimum(donor - 1, most - sink)
    moved = jax.random.randint(jax.random.fold_in(own_key, 1), (couples,), 0, 1 << 20) % (room + 1)
    sizes = sizes.at[1:1 + 2 * couples:2].set(donor - moved).at[2:2 + 2 * couples:2].set(sink + moved)
    return sizes[jax.random.permutation(jax.random.fold_in(own_key, 2), amount)]


def gaussian(rng, shape, scale, bound, pieces=(), held_as=jnp.bfloat16):
    array = jax.random.normal(rng, shape, jnp.float32) * scale
    if len(pieces) > 0:
        array = level_of(rng, shape, pieces, -0.22, 0.18) * array
    return jnp.clip(array, min=-bound, max=bound).astype(held_as)


def setup_inputs(seed: int = 0, part: int = 0) -> dict:
    key_of = jax.random.split(jax.random.key(seed), 14)
    part_keys = jax.random.split(jax.random.fold_in(key_of[13], part), 14)
    hidden = gaussian(part_keys[0], (TOKENS, D), 1.0, 6.0, ((0, 2), (1, 16)))
    out_grad = gaussian(part_keys[1], (TOKENS, D), 32.0, 192.0, ((0, 2), (1, 16)))
    norm_gain = jnp.clip(1.0 + 0.15 * jax.random.normal(key_of[2], (D,), jnp.float32), 0.25, 1.75)
    w_query = gaussian(key_of[3], (D, HEADS * HEAD), D ** -0.5, 0.0625, ((1, 16),))
    w_key = gaussian(key_of[4], (D, KV, HEAD), (D // 9) ** -0.5, 0.1875, ((2, 16),))
    w_value = gaussian(key_of[5], (D, KV, HEAD), D ** -0.5, 0.0625, ((2, 16),))
    w_out = gaussian(key_of[6], (HEADS * HEAD, D), (HEADS * HEAD) ** -0.5, 0.125, ((0, 16),))
    cache_keys = draw_cache_keys(jax.random.fold_in(jax.random.fold_in(key_of[13], part), 71), part)
    cache_values = gaussian(part_keys[8], (CACHE_LEN, KV * HEAD), 1.0, 6.0, ((0, 32),), jnp.float32)
    first_moment = gaussian(part_keys[9], (2, CACHE_LEN, KV * HEAD), 0.03, 0.1875, ((1, 32),), jnp.float32)
    second_moment = jnp.clip(jnp.exp(math.log(0.002) - 2.9957323 * jax.random.uniform(part_keys[10], (2, CACHE_LEN, KV * HEAD), jnp.float32) ** level_of(part_keys[10], (2, CACHE_LEN, KV * HEAD), ((1, 32),), -0.2, 0.2)), 0.0001, 0.002)
    conv_lengths = jax.vmap(lambda own: ragged(own, CONV, TOK_DEV, CONV_MOST, 2))(jax.random.split(part_keys[11], N_DP)).reshape((N_DP, CONV)).astype(jnp.int32)
    row_offsets = touch_ends(jax.random.randint(part_keys[12], (N_DP, CONV), 0, OFFSET_MAX), jax.random.fold_in(part_keys[12], 1), 0, OFFSET_MAX - 1).astype(jnp.int32)
    return dict(hidden=hidden, out_grad=out_grad, norm_gain=norm_gain, w_query=w_query, w_key=w_key, w_value=w_value, w_out=w_out, cache_keys=cache_keys, cache_values=cache_values, first_moment=first_moment, second_moment=second_moment, conv_lengths=conv_lengths, row_offsets=row_offsets)


THETA = 500000.0
BETA_ONE = 0.9
BETA_TWO = 0.999
RATE = 0.02
EPSILON = 1e-08

def rope_tables(position, head_width):
    half_width = head_width // 2
    inverse = jnp.exp(jnp.arange(half_width, dtype=jnp.float32) * (-2.0 * math.log(THETA) / head_width))
    angles = position.astype(jnp.float32)[:, None] * inverse[None, :]
    return (jnp.cos(angles), jnp.sin(angles))

def rotate(tensor, cos_table, sin_table):
    half_width = tensor.shape[1] // 2
    first_half = tensor[:, :half_width]
    second_half = tensor[:, half_width:]
    return jnp.concatenate([first_half * cos_table - second_half * sin_table, second_half * cos_table + first_half * sin_table], axis=1)

def row_layout(lengths, offsets, row_count, cache_len):
    end_rows = jnp.cumsum(lengths).astype(jnp.int32)
    start_rows = end_rows - lengths
    row_index = jnp.arange(row_count, dtype=jnp.int32)
    segment = lax.optimization_barrier(jnp.sum((row_index[:, None] >= end_rows[None, :]).astype(jnp.int32), axis=1))
    onehot = segment[:, None] == jnp.arange(lengths.shape[0], dtype=jnp.int32)[None, :]
    first_row = lax.optimization_barrier(jnp.sum(jnp.where(onehot, start_rows[None, :], 0), axis=1))
    offset_row = lax.optimization_barrier(jnp.sum(jnp.where(onehot, offsets[None, :], 0), axis=1))
    return (segment, cache_len + offset_row + row_index - first_row)

def attend(query, grad_out, cache_k, cache_v, self_k, self_v, allowed, score_scale):
    contract = (((1,), (1,)), ((), ()))
    score_cache = lax.dot_general(query, cache_k, contract, preferred_element_type=jnp.float32) * score_scale
    score_self = lax.dot_general(query, self_k, contract, preferred_element_type=jnp.float32) * score_scale
    score_self = jnp.where(allowed, score_self, -1e+30)
    highest = jnp.maximum(lax.optimization_barrier(jnp.max(score_cache, axis=1, keepdims=True)), lax.optimization_barrier(jnp.max(score_self, axis=1, keepdims=True)))
    exp_cache = jnp.exp(score_cache - highest)
    exp_self = jnp.exp(score_self - highest)
    denominator = lax.optimization_barrier(jnp.sum(exp_cache, axis=1, keepdims=True)) + lax.optimization_barrier(jnp.sum(exp_self, axis=1, keepdims=True))
    prob_cache = exp_cache / denominator
    prob_self = exp_self / denominator
    weight_cache = prob_cache.astype(jnp.bfloat16)
    weight_self = prob_self.astype(jnp.bfloat16)
    attended = jnp.dot(weight_cache, cache_v, preferred_element_type=jnp.float32) + jnp.dot(weight_self, self_v, preferred_element_type=jnp.float32)
    delta_row = lax.optimization_barrier(jnp.sum(grad_out.astype(jnp.float32) * attended, axis=1, keepdims=True))
    grad_prob = lax.dot_general(grad_out, cache_v, contract, preferred_element_type=jnp.float32)
    grad_score = (prob_cache * (grad_prob - delta_row)).astype(jnp.bfloat16)
    return (grad_score, weight_cache)

def adam_update(master, gradient, first, second):
    first_new = BETA_ONE * first + (1.0 - BETA_ONE) * gradient
    second_new = BETA_TWO * second + (1.0 - BETA_TWO) * gradient * gradient
    first_hat = first_new / (1.0 - BETA_ONE ** ADAM_STEP)
    second_hat = second_new / (1.0 - BETA_TWO ** ADAM_STEP)
    return (master - RATE * first_hat / (jnp.sqrt(second_hat) + EPSILON), first_new, second_new)

def reference(hidden, out_grad, norm_gain, w_query, w_key, w_value, w_out, cache_keys, cache_values, first_moment, second_moment, conv_lengths, row_offsets):
    groups = HEADS // KV
    score_scale = HEAD ** (-0.5)
    hidden_f = hidden.astype(jnp.float32)
    inv_rms = lax.rsqrt(lax.optimization_barrier(jnp.mean(hidden_f * hidden_f, axis=1, keepdims=True)) + 1e-05)
    normed = (hidden_f * inv_rms * norm_gain).astype(jnp.bfloat16)

    def layout_one(lengths, offsets):
        return row_layout(lengths, offsets, TOK_DEV, CACHE_LEN)
    segment, position = jax.vmap(layout_one)(conv_lengths, row_offsets)
    segment = (segment + CONV * jnp.arange(N_DP, dtype=jnp.int32)[:, None]).reshape(TOKENS)
    position = position.reshape(TOKENS)
    cos_table, sin_table = rope_tables(position, HEAD)
    row_index = jnp.arange(TOKENS, dtype=jnp.int32)
    allowed = (segment[:, None] == segment[None, :]) & (row_index[None, :] <= row_index[:, None])
    key_matrix = w_key.reshape(D, KV * HEAD)
    value_matrix = w_value.reshape(D, KV * HEAD)
    keys_raw = jnp.dot(normed, key_matrix, preferred_element_type=jnp.float32).astype(jnp.bfloat16)
    values_self = jnp.dot(normed, value_matrix, preferred_element_type=jnp.float32).astype(jnp.bfloat16)
    cache_k = cache_keys.astype(jnp.bfloat16)
    cache_v = cache_values.astype(jnp.bfloat16)

    def one_head(head_index):
        kv_head = head_index // groups
        w_head = lax.dynamic_slice_in_dim(w_query, head_index * HEAD, HEAD, 1)
        query = rotate(jnp.dot(normed, w_head, preferred_element_type=jnp.float32), cos_table, sin_table).astype(jnp.bfloat16)
        out_rows = lax.dynamic_slice_in_dim(w_out, head_index * HEAD, HEAD, 0)
        grad_out = lax.dot_general(out_grad, out_rows, (((1,), (1,)), ((), ())), preferred_element_type=jnp.float32).astype(jnp.bfloat16)
        self_k = rotate(lax.dynamic_slice_in_dim(keys_raw, kv_head * HEAD, HEAD, 1).astype(jnp.float32), cos_table, sin_table).astype(jnp.bfloat16)
        self_v = lax.dynamic_slice_in_dim(values_self, kv_head * HEAD, HEAD, 1)
        head_k = lax.dynamic_slice_in_dim(cache_k, kv_head * HEAD, HEAD, 1)
        head_v = lax.dynamic_slice_in_dim(cache_v, kv_head * HEAD, HEAD, 1)
        grad_score, weight_cache = attend(query, grad_out, head_k, head_v, self_k, self_v, allowed, score_scale)
        score_split = grad_score.astype(jnp.float32).reshape(N_DP, TOK_DEV, CACHE_LEN)
        query_split = query.astype(jnp.float32).reshape(N_DP, TOK_DEV, HEAD)
        key_part = (jnp.einsum('nts,nth->nsh', score_split, query_split) * score_scale).astype(jnp.bfloat16)
        weight_split = weight_cache.astype(jnp.float32).reshape(N_DP, TOK_DEV, CACHE_LEN)
        grad_split = grad_out.astype(jnp.float32).reshape(N_DP, TOK_DEV, HEAD)
        value_part = jnp.einsum('nts,nth->nsh', weight_split, grad_split).astype(jnp.bfloat16)
        return (key_part, value_part)
    key_parts, value_parts = lax.map(one_head, jnp.arange(HEADS, dtype=jnp.int32))

    def collect(parts):
        summed = parts.astype(jnp.float32).reshape(KV, groups * N_DP, CACHE_LEN, HEAD).sum(axis=1)
        return summed.transpose(1, 0, 2).reshape(CACHE_LEN, KV * HEAD)
    gradient = jnp.stack([collect(key_parts), collect(value_parts)])
    master = jnp.stack([cache_keys, cache_values])
    new_master, first_new, second_new = adam_update(master, gradient, first_moment, second_moment)
    return (new_master[0], new_master[1], first_new, second_new)
```

```python
import math

import jax
import jax.numpy as jnp
from jax import lax
from jax.experimental import pallas as pl
from jax.experimental.pallas import tpu as pltpu
from jax.sharding import PartitionSpec as P

KV = 8
ADAM_STEP = 10


THETA = 500000.0
BETA_ONE = 0.9
BETA_TWO = 0.999
RATE = 0.02
EPSILON = 1e-08


def rope_tables(position, head_width):
    half_width = head_width // 2
    inverse = jnp.exp(
        jnp.arange(half_width, dtype=jnp.float32) * (-2.0 * math.log(THETA) / head_width)
    )
    angles = position.astype(jnp.float32)[:, None] * inverse[None, :]
    return (jnp.cos(angles), jnp.sin(angles))


def rotate(tensor, cos_table, sin_table):
    half_width = tensor.shape[1] // 2
    first_half = tensor[:, :half_width]
    second_half = tensor[:, half_width:]
    return jnp.concatenate(
        [
            first_half * cos_table - second_half * sin_table,
            second_half * cos_table + first_half * sin_table,
        ],
        axis=1,
    )


def row_layout(lengths, offsets, row_count, cache_len):
    end_rows = jnp.cumsum(lengths)
    start_rows = end_rows - lengths
    row_index = jnp.arange(row_count, dtype=jnp.int32)
    segment = jnp.sum((row_index[:, None] >= end_rows[None, :]).astype(jnp.int32), axis=1)
    onehot = segment[:, None] == jnp.arange(lengths.shape[0], dtype=jnp.int32)[None, :]
    first_row = jnp.sum(jnp.where(onehot, start_rows[None, :], 0), axis=1)
    offset_row = jnp.sum(jnp.where(onehot, offsets[None, :], 0), axis=1)
    return (segment, cache_len + offset_row + row_index - first_row)


def attend(query, grad_out, cache_k, cache_v, self_k, self_v, allowed, score_scale):
    contract = (((1,), (1,)), ((), ()))
    score_cache = (
        lax.dot_general(query, cache_k, contract, preferred_element_type=jnp.float32) * score_scale
    )
    score_self = (
        lax.dot_general(query, self_k, contract, preferred_element_type=jnp.float32) * score_scale
    )
    score_self = jnp.where(allowed, score_self, -1e30)
    highest = jnp.maximum(
        jnp.max(score_cache, axis=1, keepdims=True), jnp.max(score_self, axis=1, keepdims=True)
    )
    exp_cache = jnp.exp(score_cache - highest)
    exp_self = jnp.exp(score_self - highest)
    denominator = jnp.sum(exp_cache, axis=1, keepdims=True) + jnp.sum(
        exp_self, axis=1, keepdims=True
    )
    prob_cache = exp_cache / denominator
    prob_self = exp_self / denominator
    weight_cache = prob_cache.astype(jnp.bfloat16)
    weight_self = prob_self.astype(jnp.bfloat16)
    attended = jnp.dot(weight_cache, cache_v, preferred_element_type=jnp.float32) + jnp.dot(
        weight_self, self_v, preferred_element_type=jnp.float32
    )
    delta_row = jnp.sum(grad_out.astype(jnp.float32) * attended, axis=1, keepdims=True)
    grad_prob = lax.dot_general(grad_out, cache_v, contract, preferred_element_type=jnp.float32)
    grad_score = (prob_cache * (grad_prob - delta_row)).astype(jnp.bfloat16)
    return (grad_score, weight_cache)


def adam_update(master, gradient, first, second):
    first_new = BETA_ONE * first + (1.0 - BETA_ONE) * gradient
    second_new = BETA_TWO * second + (1.0 - BETA_TWO) * gradient * gradient
    first_hat = first_new / (1.0 - BETA_ONE**ADAM_STEP)
    second_hat = second_new / (1.0 - BETA_TWO**ADAM_STEP)
    return (master - RATE * first_hat / (jnp.sqrt(second_hat) + EPSILON), first_new, second_new)


def source_total(pieces):
    head_width = pieces.shape[2]
    item_count = pieces.shape[1]
    summed = (
        pieces.astype(jnp.float32)
        .reshape(KV, pieces.shape[0] // KV, item_count, head_width)
        .sum(axis=1)
    )
    return summed.transpose(1, 0, 2).reshape(item_count, KV * head_width)


def totals_pair(pieces):
    return (source_total(pieces[0]), source_total(pieces[1]))


def per_device(
    hidden,
    out_grad,
    norm_gain,
    w_query,
    w_key,
    w_value,
    w_out,
    cache_keys,
    cache_values,
    first_moment,
    second_moment,
    conv_lengths,
    row_offsets,
):
    cache_count = lax.axis_size("cache")
    data_count = lax.axis_size("dp")
    pos_count = cache_keys.shape[0]
    device_count = cache_count * data_count
    cache_len = pos_count * device_count
    head_width = w_query.shape[1]
    column_share = w_key.shape[2]
    groups = cache_count // KV
    kv_head = lax.axis_index("cache") // groups
    score_scale = head_width ** (-0.5)
    hidden_full, grad_full = (
        lax.all_gather(hidden, "cache", axis=1, tiled=True),
        lax.all_gather(out_grad, "cache", axis=1, tiled=True),
    )
    row_count = hidden_full.shape[0]
    width_full = hidden_full.shape[1]
    hidden_f = hidden_full.astype(jnp.float32)
    inv_rms = lax.rsqrt(jnp.mean(hidden_f * hidden_f, axis=1, keepdims=True) + 1e-05)
    normed = (hidden_f * inv_rms * norm_gain).astype(jnp.bfloat16)
    segment, position = row_layout(conv_lengths[0], row_offsets[0], row_count, cache_len)
    cos_table, sin_table = rope_tables(position, head_width)
    query = rotate(
        jnp.dot(normed, w_query, preferred_element_type=jnp.float32), cos_table, sin_table
    ).astype(jnp.bfloat16)
    key_piece = (
        jnp.dot(
            normed, w_key.reshape(width_full, KV * column_share), preferred_element_type=jnp.float32
        )
        .astype(jnp.bfloat16)
        .reshape(row_count, KV, column_share)
    )
    value_piece = (
        jnp.dot(
            normed,
            w_value.reshape(width_full, KV * column_share),
            preferred_element_type=jnp.float32,
        )
        .astype(jnp.bfloat16)
        .reshape(row_count, KV, column_share)
    )
    keys_raw, values_self = (
        lax.all_gather(key_piece, "cache", axis=2, tiled=True),
        lax.all_gather(value_piece, "cache", axis=2, tiled=True),
    )
    own_keys = lax.dynamic_slice_in_dim(keys_raw, kv_head, 1, 1).reshape(row_count, head_width)
    self_k = rotate(own_keys.astype(jnp.float32), cos_table, sin_table).astype(jnp.bfloat16)
    self_v = lax.dynamic_slice_in_dim(values_self, kv_head, 1, 1).reshape(row_count, head_width)
    grad_out = lax.dot_general(
        grad_full, w_out, (((1,), (1,)), ((), ())), preferred_element_type=jnp.float32
    ).astype(jnp.bfloat16)
    cache_k = cache_keys.astype(jnp.bfloat16)
    cache_v = cache_values.astype(jnp.bfloat16)
    keys_all, values_all = (
        lax.all_gather(cache_k, ("cache", "dp"), axis=0, tiled=True),
        lax.all_gather(cache_v, ("cache", "dp"), axis=0, tiled=True),
    )
    head_k = lax.dynamic_slice_in_dim(keys_all, kv_head * head_width, head_width, 1)
    head_v = lax.dynamic_slice_in_dim(values_all, kv_head * head_width, head_width, 1)
    row_index = jnp.arange(row_count, dtype=jnp.int32)
    allowed = (segment[:, None] == segment[None, :]) & (row_index[None, :] <= row_index[:, None])
    grad_score, weight_cache = attend(
        query, grad_out, head_k, head_v, self_k, self_v, allowed, score_scale
    )
    transposed = (((0,), (0,)), ((), ()))
    key_part = (
        lax.dot_general(grad_score, query, transposed, preferred_element_type=jnp.float32)
        * score_scale
    ).astype(jnp.bfloat16)
    value_part = lax.dot_general(
        weight_cache, grad_out, transposed, preferred_element_type=jnp.float32
    ).astype(jnp.bfloat16)
    send_k = key_part.reshape(device_count, pos_count, head_width)
    send_v = value_part.reshape(device_count, pos_count, head_width)
    grad_k, grad_v = totals_pair(
        (
            lax.all_to_all(send_k, ("cache", "dp"), split_axis=0, concat_axis=0, tiled=True),
            lax.all_to_all(send_v, ("cache", "dp"), split_axis=0, concat_axis=0, tiled=True),
        )
    )
    gradient = jnp.stack([grad_k, grad_v])
    master = jnp.stack([cache_keys, cache_values])
    new_master, first_new, second_new = adam_update(master, gradient, first_moment, second_moment)
    return (new_master[0], new_master[1], first_new, second_new)


LINE = 4
PLANE = 4
MESH = pl.DeviceIdType.MESH


def fits(mesh):
    return mesh.shape["cache"] == LINE * PLANE and mesh.shape["dp"] == 2


def fused_kernel(
    hid,
    og,
    ss_in,
    gain,
    wqkv,
    wout,
    ckv,
    cosd,
    sind,
    cos_t,
    sin_t,
    mask_t,
    eye,
    ck,
    cv,
    fm,
    sm,
    nk,
    nv,
    nf,
    ns,
    hbuf,
    obuf,
    srecv,
    wbuf,
    wobuf,
    cbuf,
    cpart,
    crecv,
    dpart,
    drecv,
    kvt,
    kvr,
    gsend,
    grecv,
    h_s,
    h_r,
    o_s,
    o_r,
    s_s,
    s_r,
    w_s,
    w_r,
    wf_s,
    wf_r,
    wo_s,
    wo_r,
    wof_s,
    wof_r,
    c_s,
    c_r,
    rc_s,
    rc_r,
    rd_s,
    rd_r,
    kv_s,
    kv_r,
    g_s,
    g_r,
    loc,
    loco,
):
    chips = LINE * PLANE
    devs = 2 * chips
    m = lax.axis_index("cache")
    c = lax.axis_index("dp")
    i = m * 2 + c
    line, p = m // PLANE, m % PLANE
    width = hid.shape[1]
    pair = LINE // 2
    mine = c * pair
    other = (1 - c) * pair
    f32, bf16 = jnp.float32, jnp.bfloat16

    barrier = pltpu.get_barrier_semaphore()

    def greet(k, carry):
        j = (i + k) % devs
        pl.semaphore_signal(
            barrier, inc=1, device_id={"cache": j // 2, "dp": j % 2}, device_id_type=MESH
        )
        return carry

    lax.fori_loop(1, devs, greet, 0)

    own_w = pltpu.make_async_copy(wqkv.at[:, p], wbuf.at[0], loc.at[0])
    own_w.start()
    own_wo = []
    for zz in range(LINE):
        col = pl.multiple_of((zz * PLANE + p) * width, width)
        cp = pltpu.make_async_copy(wout.at[:, pl.ds(col, width)], wobuf.at[0, zz], loco.at[zz])
        cp.start()
        own_wo.append(cp)
    own_c = pltpu.make_async_copy(ckv.at[m // (chips // KV)], cbuf.at[i], loc.at[1])
    own_c.start()
    pl.semaphore_wait(barrier, devs - 1)

    def remote(src, dst, ss, rs, chip, core):
        return pltpu.make_async_remote_copy(
            src_ref=src,
            dst_ref=dst,
            send_sem=ss,
            recv_sem=rs,
            device_id={"cache": chip, "dp": core},
            device_id_type=MESH,
        )

    def ss_copy(k):
        return remote(ss_in, srecv.at[k], s_s.at[k], s_r.at[k], (m + k) % chips, c)

    def start_ss(k, carry):
        ss_copy(k).start()
        return carry

    lax.fori_loop(1, chips, start_ss, 0)

    def line_chip(k):
        return ((line + k) % LINE) * PLANE + p

    def plane_chip(k):
        return line * PLANE + (p + k) % PLANE

    def back_chip(k):
        return line * PLANE + (p + PLANE - k) % PLANE

    o_cp, h_cp, w_cp, wo_cp = {}, {}, {}, {}
    for k in range(1, LINE):
        o_cp[k] = remote(og, obuf.at[k], o_s.at[k], o_r.at[k], line_chip(k), c)
        o_cp[k].start()
    for k in range(1, PLANE):
        for h in range(pair):
            col = pl.multiple_of(((mine + h) * PLANE + (p + k) % PLANE) * width, width)
            wo_cp[k, h] = remote(
                wout.at[:, pl.ds(col, width)],
                wobuf.at[k, mine + h],
                wo_s.at[k, h],
                wo_r.at[k, h],
                plane_chip(k),
                c,
            )
            wo_cp[k, h].start()
    for k in range(1, LINE):
        h_cp[k] = remote(hid, hbuf.at[k], h_s.at[k], h_r.at[k], line_chip(k), c)
        h_cp[k].start()
    for k in range(1, PLANE):
        w_cp[k] = remote(
            wqkv.at[pl.ds(mine, pair), (p + k) % PLANE],
            wbuf.at[k, pl.ds(mine, pair)],
            w_s.at[k],
            w_r.at[k],
            plane_chip(k),
            c,
        )
        w_cp[k].start()

    def c_copy(k):
        j = (i + k) % devs
        return remote(
            ckv.at[(j // 2) // (chips // KV)], cbuf.at[i], c_s.at[k], c_r.at[k], j // 2, j % 2
        )

    def start_c(k, carry):
        c_copy(k).start()
        return carry

    lax.fori_loop(1, devs, start_c, 0)

    wof_cp = {}
    for k in range(1, PLANE):
        for h in range(pair):
            wo_cp[k, h].wait_recv()
            wof_cp[k, h] = remote(
                wobuf.at[k, mine + h],
                wobuf.at[k, mine + h],
                wof_s.at[k, h],
                wof_r.at[k, h],
                m,
                1 - c,
            )
            wof_cp[k, h].start()
    for cp in own_wo:
        cp.wait()
    for k in range(1, PLANE):
        for h in range(pair):
            wof_cp[k, h].wait_recv()

    for kz in range(LINE):
        if kz == 0:
            block = og[...]
        else:
            o_cp[kz].wait_recv()
            block = obuf[kz]
        zz = (line + LINE - kz) % LINE

        def add_d(k, carry):
            term = lax.dot_general(
                block, wobuf[k, zz], (((1,), (1,)), ((), ())), preferred_element_type=f32
            )
            if kz == 0:
                dpart[k] = term
            else:
                dpart[k] = dpart[k] + term
            return carry

        lax.fori_loop(0, PLANE, add_d, 0)

    rd_cp = {}
    for k in range(1, PLANE):
        rd_cp[k] = remote(dpart.at[k], drecv.at[k], rd_s.at[k], rd_r.at[k], back_chip(k), c)
        rd_cp[k].start()

    wf_cp = {}
    for k in range(1, PLANE):
        w_cp[k].wait_recv()
        part = wbuf.at[k, pl.ds(mine, pair)]
        wf_cp[k] = remote(part, part, wf_s.at[k], wf_r.at[k], m, 1 - c)
        wf_cp[k].start()

    def wait_ss(k, carry):
        ss_copy(k).wait()
        return carry

    lax.fori_loop(1, chips, wait_ss, 0)
    srecv[0] = ss_in[...]
    total = jnp.sum(srecv[...], axis=0)
    spread = lax.dot_general(
        total,
        jnp.full((8, 128), 0.125, f32),
        (((0,), (0,)), ((), ())),
        preferred_element_type=f32,
        precision=lax.Precision.HIGHEST,
    )
    inv = lax.rsqrt(spread[:, :1] * (1.0 / (width * chips)) + 1e-05)
    own_w.wait()
    for k in range(1, PLANE):
        wf_cp[k].wait_recv()
    for kz in range(LINE):
        zz = (line + LINE - kz) % LINE
        if kz == 0:
            block = hid[...]
        else:
            h_cp[kz].wait_recv()
            block = hbuf[kz]
        normed = (block.astype(f32) * inv * gain[zz * PLANE + p]).astype(bf16)

        def add_c(k, carry):
            term = jnp.dot(normed, wbuf[k, zz], preferred_element_type=f32)
            if kz == 0:
                cpart[k] = term
            else:
                cpart[k] = cpart[k] + term
            return carry

        lax.fori_loop(0, PLANE, add_c, 0)

    rc_cp = {}
    for k in range(1, PLANE):
        rc_cp[k] = remote(cpart.at[k], crecv.at[k], rc_s.at[k], rc_r.at[k], back_chip(k), c)
        rc_cp[k].start()

    grad = dpart[0]
    for k in range(1, PLANE):
        rd_cp[k].wait_recv()
        grad = grad + drecv[k]
    grad = grad.astype(bf16)
    grad_t = lax.dot_general(
        eye[...], grad, (((1,), (1,)), ((), ())), preferred_element_type=f32
    )
    own_c.wait()

    def wait_c(k, carry):
        c_copy(k).wait()
        return carry

    lax.fori_loop(1, devs, wait_c, 0)
    rows = ck.shape[0]
    cache_len = rows * devs
    head_k = cbuf[:, :rows, :].reshape(cache_len, 128)
    head_v = cbuf[:, rows:, :].reshape(cache_len, 128)
    grad_prob = lax.dot_general(
        head_v, grad, (((1,), (1,)), ((), ())), preferred_element_type=f32
    )

    qkv = cpart[0]
    for k in range(1, PLANE):
        rc_cp[k].wait_recv()
        qkv = qkv + crecv[k]
    kv = qkv[:, 128:].astype(bf16)
    kvt[...] = lax.dot_general(
        eye[...], kv, (((1,), (1,)), ((), ())), preferred_element_type=f32
    ).astype(bf16)

    def kv_part(chip):
        return kvt.at[pl.ds(pl.multiple_of((chip // (chips // KV)) * 16, 16), 16)]

    def kv_copy(k):
        j = (m + k) % chips
        return remote(kv_part(j), kvr.at[m], kv_s.at[k], kv_r.at[k], j, c)

    def start_kv(k, carry):
        kv_copy(k).start()
        return carry

    lax.fori_loop(1, chips, start_kv, 0)
    own_kv = pltpu.make_async_copy(kv_part(m), kvr.at[m], loc.at[2])
    own_kv.start()

    scale = 128 ** (-0.5)
    q_raw = qkv[:, :128]
    turned = jnp.concatenate([q_raw[:, 64:], q_raw[:, :64]], axis=1)
    query = (q_raw * cosd[...] + turned * sind[...]).astype(bf16)
    query_t = lax.dot_general(
        eye[...], query, (((1,), (1,)), ((), ())), preferred_element_type=f32
    ).astype(bf16)
    score = jnp.dot(head_k, query_t, preferred_element_type=f32) * scale
    top = jnp.max(score, axis=0, keepdims=True)

    def wait_kv(k, carry):
        kv_copy(k).wait()
        return carry

    lax.fori_loop(1, chips, wait_kv, 0)
    own_kv.wait()
    kvf = kvr[...].astype(f32)
    key_t = kvf[:, :8, :].reshape(128, kvf.shape[2])
    value_t = kvf[:, 8:, :].reshape(128, kvf.shape[2]).astype(bf16)
    turned_t = jnp.concatenate([key_t[64:], key_t[:64]], axis=0)
    key_t = (key_t * cos_t[...] + turned_t * sin_t[...]).astype(bf16)
    score_self = (
        lax.dot_general(key_t, query_t, (((0,), (0,)), ((), ())), preferred_element_type=f32)
        * scale
    )
    score_self = jnp.where(mask_t[...] > 0.5, score_self, -1e30)
    top = jnp.maximum(top, jnp.max(score_self, axis=0, keepdims=True))
    e_cache = jnp.exp(score - top)
    e_self = jnp.exp(score_self - top)
    inverse = 1.0 / (
        jnp.sum(e_cache, axis=0, keepdims=True) + jnp.sum(e_self, axis=0, keepdims=True)
    )
    prob = e_cache * inverse
    weight = prob.astype(bf16)
    weight_self = (e_self * inverse).astype(bf16)
    attended = lax.dot_general(
        head_v, weight, (((0,), (0,)), ((), ())), preferred_element_type=f32
    ) + jnp.dot(value_t, weight_self, preferred_element_type=f32)
    delta = jnp.sum(grad_t * attended, axis=0, keepdims=True)
    grad_score = (prob * (grad_prob - delta)).astype(bf16)
    value_part = jnp.dot(weight, grad, preferred_element_type=f32).astype(bf16)
    key_part = (jnp.dot(grad_score, query, preferred_element_type=f32) * scale).astype(bf16)
    gsend[:, :rows, :] = key_part.reshape(devs, rows, 128)
    gsend[:, rows:, :] = value_part.reshape(devs, rows, 128)

    def g_copy(k):
        j = (i + k) % devs
        return remote(gsend.at[j], grecv.at[i], g_s.at[k], g_r.at[k], j // 2, j % 2)

    def start_g(k, carry):
        g_copy(k).start()
        return carry

    lax.fori_loop(1, devs, start_g, 0)
    own_g = pltpu.make_async_copy(gsend.at[i], grecv.at[i], loc.at[3])
    own_g.start()

    for k in range(1, LINE):
        o_cp[k].wait_send()
        h_cp[k].wait_send()
    for k in range(1, PLANE):
        w_cp[k].wait_send()
        wf_cp[k].wait_send()
        rd_cp[k].wait_send()
        rc_cp[k].wait_send()
        for h in range(pair):
            wo_cp[k, h].wait_send()
            wof_cp[k, h].wait_send()

    def wait_g(k, carry):
        g_copy(k).wait()
        return carry

    lax.fori_loop(1, devs, wait_g, 0)
    own_g.wait()

    share = devs // KV
    for g in range(KV):
        got = jnp.sum(grecv[g * share : (g + 1) * share].astype(f32), axis=0)
        cols = slice(g * 128, (g + 1) * 128)
        for which, master, out in ((0, ck, nk), (1, cv, nv)):
            gradient = got[which * rows : (which + 1) * rows]
            new, first, second = adam_update(
                master[:, cols], gradient, fm[which, :, cols], sm[which, :, cols]
            )
            out[:, cols] = new
            nf[which, :, cols] = first
            ns[which, :, cols] = second


def fused_device(
    hidden,
    out_grad,
    norm_gain,
    w_query,
    w_key,
    w_value,
    w_out,
    cache_keys,
    cache_values,
    first_moment,
    second_moment,
    conv_lengths,
    row_offsets,
):
    chips = LINE * PLANE
    devs = 2 * chips
    f32, bf16 = jnp.float32, jnp.bfloat16
    rows, width = hidden.shape
    pos = cache_keys.shape[0]
    cache_len = pos * devs
    head = w_query.shape[1]
    full = w_query.shape[0]
    hf = hidden.astype(f32)
    squares = jnp.broadcast_to(jnp.sum(hf * hf, axis=1)[None, :], (8, rows))
    w_kv = jnp.stack([w_key, w_value], axis=2).reshape(full, head)
    wqkv = jnp.concatenate([w_query, w_kv], axis=1).reshape(LINE, PLANE, width, 2 * head)
    ckv = jnp.stack(
        [cache_keys.astype(bf16).reshape(pos, KV, head), cache_values.astype(bf16).reshape(pos, KV, head)]
    )
    ckv = ckv.transpose(2, 0, 1, 3).reshape(KV, 2 * pos, head)
    segment, position = row_layout(conv_lengths[0], row_offsets[0], rows, cache_len)
    cos, sin = rope_tables(position, head)
    cosd = jnp.concatenate([cos, cos], axis=1)
    sind = jnp.concatenate([-sin, sin], axis=1)
    index = jnp.arange(rows, dtype=jnp.int32)
    mask_t = ((segment[:, None] == segment[None, :]) & (index[:, None] <= index[None, :])).astype(f32)
    eye = jnp.eye(head, dtype=bf16)
    vm = pl.BlockSpec(memory_space=pltpu.VMEM)
    hbm = pl.BlockSpec(memory_space=pl.ANY)
    dma = pltpu.SemaphoreType.DMA
    pair = LINE // 2
    out_shape = (
        jax.ShapeDtypeStruct(cache_keys.shape, f32),
        jax.ShapeDtypeStruct(cache_keys.shape, f32),
        jax.ShapeDtypeStruct(first_moment.shape, f32),
        jax.ShapeDtypeStruct(first_moment.shape, f32),
    )
    return pl.pallas_call(
        fused_kernel,
        out_shape=out_shape,
        in_specs=[vm, vm, vm, vm, hbm, hbm] + [vm] * 11,
        out_specs=(vm,) * 4,
        scratch_shapes=[
            pltpu.VMEM((LINE, rows, width), bf16),
            pltpu.VMEM((LINE, rows, width), bf16),
            pltpu.VMEM((chips, 8, rows), f32),
            pltpu.VMEM((PLANE, LINE, width, 2 * head), bf16),
            pltpu.VMEM((PLANE, LINE, head, width), bf16),
            pltpu.VMEM((devs, 2 * pos, head), bf16),
            pltpu.VMEM((PLANE, rows, 2 * head), f32),
            pltpu.VMEM((PLANE, rows, 2 * head), f32),
            pltpu.VMEM((PLANE, rows, head), f32),
            pltpu.VMEM((PLANE, rows, head), f32),
            pltpu.VMEM((head, rows), bf16),
            pltpu.VMEM((chips, 16, rows), bf16),
            pltpu.VMEM((devs, 2 * pos, head), bf16),
            pltpu.VMEM((devs, 2 * pos, head), bf16),
            dma((LINE,)),
            dma((LINE,)),
            dma((LINE,)),
            dma((LINE,)),
            dma((chips,)),
            dma((chips,)),
            dma((PLANE,)),
            dma((PLANE,)),
            dma((PLANE,)),
            dma((PLANE,)),
            dma((PLANE, pair)),
            dma((PLANE, pair)),
            dma((PLANE, pair)),
            dma((PLANE, pair)),
            dma((devs,)),
            dma((devs,)),
            dma((PLANE,)),
            dma((PLANE,)),
            dma((PLANE,)),
            dma((PLANE,)),
            dma((chips,)),
            dma((chips,)),
            dma((devs,)),
            dma((devs,)),
            dma((4,)),
            dma((LINE,)),
        ],
        compiler_params=pltpu.CompilerParams(
            collective_id=0, has_side_effects=True, vmem_limit_bytes=56 * 1024 * 1024
        ),
    )(
        hidden,
        out_grad,
        squares,
        norm_gain.reshape(chips, 1, width),
        wqkv,
        w_out,
        ckv,
        cosd,
        sind,
        cosd.T,
        sind.T,
        mask_t,
        eye,
        cache_keys,
        cache_values,
        first_moment,
        second_moment,
    )


def solution(mesh):
    return jax.shard_map(
        fused_device if fits(mesh) else per_device,
        mesh=mesh,
        in_specs=(
            P(("groups", "dp"), "cache"),
            P(("groups", "dp"), "cache"),
            P(),
            P(None, "cache"),
            P(None, None, "cache"),
            P(None, None, "cache"),
            P("cache", None),
            P(("groups", "cache", "dp"), None),
            P(("groups", "cache", "dp"), None),
            P(None, ("groups", "cache", "dp"), None),
            P(None, ("groups", "cache", "dp"), None),
            P(("groups", "dp"), None),
            P(("groups", "dp"), None),
        ),
        out_specs=(
            P(("groups", "cache", "dp"), None),
            P(("groups", "cache", "dp"), None),
            P(None, ("groups", "cache", "dp"), None),
            P(None, ("groups", "cache", "dp"), None),
        ),
        check_vma=False,
    )
```

```python
import math

import jax
import jax.numpy as jnp
from jax import lax
from jax.experimental import pallas as pl
from jax.experimental.pallas import tpu as pltpu
from jax.sharding import PartitionSpec as P

KV = 8
ADAM_STEP = 10


THETA = 500000.0
BETA_ONE = 0.9
BETA_TWO = 0.999
RATE = 0.02
EPSILON = 1e-08


def rope_tables(position, head_width):
    half_width = head_width // 2
    inverse = jnp.exp(
        jnp.arange(half_width, dtype=jnp.float32) * (-2.0 * math.log(THETA) / head_width)
    )
    angles = position.astype(jnp.float32)[:, None] * inverse[None, :]
    return (jnp.cos(angles), jnp.sin(angles))


def rotate(tensor, cos_table, sin_table):
    half_width = tensor.shape[1] // 2
    first_half = tensor[:, :half_width]
    second_half = tensor[:, half_width:]
    return jnp.concatenate(
        [
            first_half * cos_table - second_half * sin_table,
            second_half * cos_table + first_half * sin_table,
        ],
        axis=1,
    )


def row_layout(lengths, offsets, row_count, cache_len):
    end_rows = jnp.cumsum(lengths)
    start_rows = end_rows - lengths
    row_index = jnp.arange(row_count, dtype=jnp.int32)
    segment = jnp.sum((row_index[:, None] >= end_rows[None, :]).astype(jnp.int32), axis=1)
    onehot = segment[:, None] == jnp.arange(lengths.shape[0], dtype=jnp.int32)[None, :]
    first_row = jnp.sum(jnp.where(onehot, start_rows[None, :], 0), axis=1)
    offset_row = jnp.sum(jnp.where(onehot, offsets[None, :], 0), axis=1)
    return (segment, cache_len + offset_row + row_index - first_row)


def attend(query, grad_out, cache_k, cache_v, self_k, self_v, allowed, score_scale):
    contract = (((1,), (1,)), ((), ()))
    score_cache = (
        lax.dot_general(query, cache_k, contract, preferred_element_type=jnp.float32) * score_scale
    )
    score_self = (
        lax.dot_general(query, self_k, contract, preferred_element_type=jnp.float32) * score_scale
    )
    score_self = jnp.where(allowed, score_self, -1e30)
    highest = jnp.maximum(
        jnp.max(score_cache, axis=1, keepdims=True), jnp.max(score_self, axis=1, keepdims=True)
    )
    exp_cache = jnp.exp(score_cache - highest)
    exp_self = jnp.exp(score_self - highest)
    denominator = jnp.sum(exp_cache, axis=1, keepdims=True) + jnp.sum(
        exp_self, axis=1, keepdims=True
    )
    prob_cache = exp_cache / denominator
    prob_self = exp_self / denominator
    weight_cache = prob_cache.astype(jnp.bfloat16)
    weight_self = prob_self.astype(jnp.bfloat16)
    attended = jnp.dot(weight_cache, cache_v, preferred_element_type=jnp.float32) + jnp.dot(
        weight_self, self_v, preferred_element_type=jnp.float32
    )
    delta_row = jnp.sum(grad_out.astype(jnp.float32) * attended, axis=1, keepdims=True)
    grad_prob = lax.dot_general(grad_out, cache_v, contract, preferred_element_type=jnp.float32)
    grad_score = (prob_cache * (grad_prob - delta_row)).astype(jnp.bfloat16)
    return (grad_score, weight_cache)


def adam_update(master, gradient, first, second):
    first_new = BETA_ONE * first + (1.0 - BETA_ONE) * gradient
    second_new = BETA_TWO * second + (1.0 - BETA_TWO) * gradient * gradient
    first_hat = first_new / (1.0 - BETA_ONE**ADAM_STEP)
    second_hat = second_new / (1.0 - BETA_TWO**ADAM_STEP)
    return (master - RATE * first_hat / (jnp.sqrt(second_hat) + EPSILON), first_new, second_new)


def source_total(pieces):
    head_width = pieces.shape[2]
    item_count = pieces.shape[1]
    summed = (
        pieces.astype(jnp.float32)
        .reshape(KV, pieces.shape[0] // KV, item_count, head_width)
        .sum(axis=1)
    )
    return summed.transpose(1, 0, 2).reshape(item_count, KV * head_width)


def totals_pair(pieces):
    return (source_total(pieces[0]), source_total(pieces[1]))


def per_device(
    hidden,
    out_grad,
    norm_gain,
    w_query,
    w_key,
    w_value,
    w_out,
    cache_keys,
    cache_values,
    first_moment,
    second_moment,
    conv_lengths,
    row_offsets,
):
    cache_count = lax.axis_size("cache")
    data_count = lax.axis_size("dp")
    pos_count = cache_keys.shape[0]
    device_count = cache_count * data_count
    cache_len = pos_count * device_count
    head_width = w_query.shape[1]
    column_share = w_key.shape[2]
    groups = cache_count // KV
    kv_head = lax.axis_index("cache") // groups
    score_scale = head_width ** (-0.5)
    hidden_full, grad_full = (
        lax.all_gather(hidden, "cache", axis=1, tiled=True),
        lax.all_gather(out_grad, "cache", axis=1, tiled=True),
    )
    row_count = hidden_full.shape[0]
    width_full = hidden_full.shape[1]
    hidden_f = hidden_full.astype(jnp.float32)
    inv_rms = lax.rsqrt(jnp.mean(hidden_f * hidden_f, axis=1, keepdims=True) + 1e-05)
    normed = (hidden_f * inv_rms * norm_gain).astype(jnp.bfloat16)
    segment, position = row_layout(conv_lengths[0], row_offsets[0], row_count, cache_len)
    cos_table, sin_table = rope_tables(position, head_width)
    query = rotate(
        jnp.dot(normed, w_query, preferred_element_type=jnp.float32), cos_table, sin_table
    ).astype(jnp.bfloat16)
    key_piece = (
        jnp.dot(
            normed, w_key.reshape(width_full, KV * column_share), preferred_element_type=jnp.float32
        )
        .astype(jnp.bfloat16)
        .reshape(row_count, KV, column_share)
    )
    value_piece = (
        jnp.dot(
            normed,
            w_value.reshape(width_full, KV * column_share),
            preferred_element_type=jnp.float32,
        )
        .astype(jnp.bfloat16)
        .reshape(row_count, KV, column_share)
    )
    keys_raw, values_self = (
        lax.all_gather(key_piece, "cache", axis=2, tiled=True),
        lax.all_gather(value_piece, "cache", axis=2, tiled=True),
    )
    own_keys = lax.dynamic_slice_in_dim(keys_raw, kv_head, 1, 1).reshape(row_count, head_width)
    self_k = rotate(own_keys.astype(jnp.float32), cos_table, sin_table).astype(jnp.bfloat16)
    self_v = lax.dynamic_slice_in_dim(values_self, kv_head, 1, 1).reshape(row_count, head_width)
    grad_out = lax.dot_general(
        grad_full, w_out, (((1,), (1,)), ((), ())), preferred_element_type=jnp.float32
    ).astype(jnp.bfloat16)
    cache_k = cache_keys.astype(jnp.bfloat16)
    cache_v = cache_values.astype(jnp.bfloat16)
    keys_all, values_all = (
        lax.all_gather(cache_k, ("cache", "dp"), axis=0, tiled=True),
        lax.all_gather(cache_v, ("cache", "dp"), axis=0, tiled=True),
    )
    head_k = lax.dynamic_slice_in_dim(keys_all, kv_head * head_width, head_width, 1)
    head_v = lax.dynamic_slice_in_dim(values_all, kv_head * head_width, head_width, 1)
    row_index = jnp.arange(row_count, dtype=jnp.int32)
    allowed = (segment[:, None] == segment[None, :]) & (row_index[None, :] <= row_index[:, None])
    grad_score, weight_cache = attend(
        query, grad_out, head_k, head_v, self_k, self_v, allowed, score_scale
    )
    transposed = (((0,), (0,)), ((), ()))
    key_part = (
        lax.dot_general(grad_score, query, transposed, preferred_element_type=jnp.float32)
        * score_scale
    ).astype(jnp.bfloat16)
    value_part = lax.dot_general(
        weight_cache, grad_out, transposed, preferred_element_type=jnp.float32
    ).astype(jnp.bfloat16)
    send_k = key_part.reshape(device_count, pos_count, head_width)
    send_v = value_part.reshape(device_count, pos_count, head_width)
    grad_k, grad_v = totals_pair(
        (
            lax.all_to_all(send_k, ("cache", "dp"), split_axis=0, concat_axis=0, tiled=True),
            lax.all_to_all(send_v, ("cache", "dp"), split_axis=0, concat_axis=0, tiled=True),
        )
    )
    gradient = jnp.stack([grad_k, grad_v])
    master = jnp.stack([cache_keys, cache_values])
    new_master, first_new, second_new = adam_update(master, gradient, first_moment, second_moment)
    return (new_master[0], new_master[1], first_new, second_new)


LINE = 4
PLANE = 4
MESH = pl.DeviceIdType.MESH


def fits(mesh):
    return mesh.shape["cache"] == LINE * PLANE and mesh.shape["dp"] == 2


def fused_kernel(
    hid,
    og,
    gain,
    wq,
    wkv,
    wout,
    ckv,
    cosd,
    sind,
    lengths,
    total_grad,
    hbuf,
    obuf,
    ss_in,
    srecv,
    wbuf,
    wkbuf,
    wobuf,
    cbuf,
    cpart,
    crecv,
    dpart,
    drecv,
    kvt,
    kvr,
    gsend,
    grecv,
    h_s,
    h_r,
    o_s,
    o_r,
    s_s,
    s_r,
    w_s,
    w_r,
    wf_s,
    wf_r,
    wk_s,
    wk_r,
    wkf_s,
    wkf_r,
    wo_s,
    wo_r,
    wof_s,
    wof_r,
    c_s,
    c_r,
    rc_s,
    rc_r,
    rd_s,
    rd_r,
    kv_s,
    kv_r,
    g_s,
    g_r,
    loc,
    loco,
):
    chips = LINE * PLANE
    devs = 2 * chips
    m = lax.axis_index("cache")
    c = lax.axis_index("dp")
    i = m * 2 + c
    line, p = m // PLANE, m % PLANE
    width = hid.shape[1]
    pair = LINE // 2
    mine = c * pair
    other = (1 - c) * pair
    f32, bf16 = jnp.float32, jnp.bfloat16

    barrier = pltpu.get_barrier_semaphore()

    def greet(k, carry):
        j = (i + k) % devs
        pl.semaphore_signal(
            barrier, inc=1, device_id={"cache": j // 2, "dp": j % 2}, device_id_type=MESH
        )
        return carry

    lax.fori_loop(1, devs, greet, 0)

    own_w = pltpu.make_async_copy(wq.at[:, p], wbuf.at[0], loc.at[0])
    own_w.start()
    own_wo = []
    for zz in range(LINE):
        col = pl.multiple_of((zz * PLANE + p) * width, width)
        cp = pltpu.make_async_copy(wout.at[:, pl.ds(col, width)], wobuf.at[0, zz], loco.at[zz])
        cp.start()
        own_wo.append(cp)
        cp = pltpu.make_async_copy(
            wkv.at[:, pl.ds(col, width)], wkbuf.at[0, zz], loco.at[LINE + zz]
        )
        cp.start()
        own_wo.append(cp)
    own_c = pltpu.make_async_copy(ckv.at[m // (chips // KV)], cbuf.at[i], loc.at[1])
    own_c.start()
    own_f = hid[...].astype(f32)
    ss_in[...] = lax.dot_general(
        jnp.ones((8, width), f32),
        own_f * own_f,
        (((1,), (1,)), ((), ())),
        preferred_element_type=f32,
        precision=lax.Precision.HIGHEST,
    )
    pl.semaphore_wait(barrier, devs - 1)

    def remote(src, dst, ss, rs, chip, core):
        return pltpu.make_async_remote_copy(
            src_ref=src,
            dst_ref=dst,
            send_sem=ss,
            recv_sem=rs,
            device_id={"cache": chip, "dp": core},
            device_id_type=MESH,
        )

    def ss_copy(k):
        return remote(ss_in, srecv.at[k], s_s.at[k], s_r.at[k], (m + k) % chips, c)

    def start_ss(k, carry):
        ss_copy(k).start()
        return carry

    lax.fori_loop(1, chips, start_ss, 0)

    def line_chip(k):
        return ((line + k) % LINE) * PLANE + p

    def plane_chip(k):
        return line * PLANE + (p + k) % PLANE

    def back_chip(k):
        return line * PLANE + (p + PLANE - k) % PLANE

    inner = jnp.logical_and(line > 0, line < LINE - 1)

    def direct(k):
        if k == LINE - 1:
            return line != 0
        if k == 1:
            return line != LINE - 1
        return None

    def when(cond, act):
        if cond is None:
            act()
        else:
            pl.when(cond)(act)

    def relay(buf, ss, rs):
        slot = 2 * line - 1
        return remote(
            buf.at[2], buf.at[slot], ss.at[0], rs.at[slot], 3 * (line - 1) * PLANE + p, c
        )

    o_cp, h_cp, w_cp, wo_cp, wk_cp = {}, {}, {}, {}, {}
    for k in (2, 1, 3):
        o_cp[k] = remote(og, obuf.at[k], o_s.at[k], o_r.at[k], line_chip(k), c)
        when(direct(k), o_cp[k].start)

    def send_rows(src, buf, ss, rs, cps):
        for k in range(1, PLANE):
            for h in range(pair):
                col = pl.multiple_of(((mine + h) * PLANE + (p + k) % PLANE) * width, width)
                cps[k, h] = remote(
                    src.at[:, pl.ds(col, width)],
                    buf.at[k, mine + h],
                    ss.at[k, h],
                    rs.at[k, h],
                    plane_chip(k),
                    c,
                )
                cps[k, h].start()

    send_rows(wout, wobuf, wo_s, wo_r, wo_cp)
    for k in (2, 1, 3):
        h_cp[k] = remote(hid, hbuf.at[k], h_s.at[k], h_r.at[k], line_chip(k), c)
        when(direct(k), h_cp[k].start)
    for k in range(1, PLANE):
        w_cp[k] = remote(
            wq.at[pl.ds(mine, pair), (p + k) % PLANE],
            wbuf.at[k, pl.ds(mine, pair)],
            w_s.at[k],
            w_r.at[k],
            plane_chip(k),
            c,
        )
        w_cp[k].start()
    send_rows(wkv, wkbuf, wk_s, wk_r, wk_cp)

    def c_copy(k):
        j = (i + k) % devs
        return remote(
            ckv.at[(j // 2) // (chips // KV)], cbuf.at[i], c_s.at[k], c_r.at[k], j // 2, j % 2
        )

    def start_c(k, carry):
        c_copy(k).start()
        return carry

    lax.fori_loop(1, devs, start_c, 0)

    o_cp[2].wait_recv()

    @pl.when(inner)
    def _():
        relay(obuf, o_s, o_r).start()

    wof_cp = {}
    for k in range(1, PLANE):
        for h in range(pair):
            wo_cp[k, h].wait_recv()
            wof_cp[k, h] = remote(
                wobuf.at[k, mine + h],
                wobuf.at[k, mine + h],
                wof_s.at[k, h],
                wof_r.at[k, h],
                m,
                1 - c,
            )
            wof_cp[k, h].start()
    for cp in own_wo:
        cp.wait()
    for k in range(1, PLANE):
        for h in range(pair):
            wof_cp[k, h].wait_recv()

    for kz in range(LINE):
        if kz == 0:
            block = og[...]
        else:
            if kz != 2:
                o_cp[kz].wait_recv()
            block = obuf[kz]
        zz = (line + LINE - kz) % LINE

        def add_d(k, carry):
            term = lax.dot_general(
                block, wobuf[k, zz], (((1,), (1,)), ((), ())), preferred_element_type=f32
            )
            if kz == 0:
                dpart[k] = term
            else:
                dpart[k] = dpart[k] + term
            return carry

        lax.fori_loop(0, PLANE, add_d, 0)

    rd_cp = {}
    for k in range(1, PLANE):
        rd_cp[k] = remote(dpart.at[k], drecv.at[k], rd_s.at[k], rd_r.at[k], back_chip(k), c)
        rd_cp[k].start()

    h_cp[2].wait_recv()

    @pl.when(inner)
    def _():
        relay(hbuf, h_s, h_r).start()

    wf_cp, wkf_cp = {}, {}
    for k in range(1, PLANE):
        w_cp[k].wait_recv()
        part = wbuf.at[k, pl.ds(mine, pair)]
        wf_cp[k] = remote(part, part, wf_s.at[k], wf_r.at[k], m, 1 - c)
        wf_cp[k].start()
        for h in range(pair):
            wk_cp[k, h].wait_recv()
            part = wkbuf.at[k, mine + h]
            wkf_cp[k, h] = remote(part, part, wkf_s.at[k, h], wkf_r.at[k, h], m, 1 - c)
            wkf_cp[k, h].start()

    unit = (
        lax.broadcasted_iota(jnp.int32, (128, 128), 0)
        == lax.broadcasted_iota(jnp.int32, (128, 128), 1)
    ).astype(f32)
    eye = unit.astype(bf16)

    def flip(table):
        return lax.dot_general(
            unit,
            table,
            (((1,), (1,)), ((), ())),
            preferred_element_type=f32,
            precision=lax.Precision.HIGHEST,
        )

    cos_t, sin_t = flip(cosd[...]), flip(sind[...])

    def wait_ss(k, carry):
        ss_copy(k).wait()
        return carry

    lax.fori_loop(1, chips, wait_ss, 0)
    srecv[0] = ss_in[...]
    total = jnp.sum(srecv[...], axis=0)
    spread = lax.dot_general(
        total,
        jnp.full((8, 128), 0.125, f32),
        (((0,), (0,)), ((), ())),
        preferred_element_type=f32,
        precision=lax.Precision.HIGHEST,
    )
    inv = lax.rsqrt(spread[:, :1] * (1.0 / (width * chips)) + 1e-05)
    own_w.wait()
    for k in range(1, PLANE):
        wf_cp[k].wait_recv()
        for h in range(pair):
            wkf_cp[k, h].wait_recv()
    for kz in range(LINE):
        zz = (line + LINE - kz) % LINE
        if kz == 0:
            block = hid[...]
        else:
            if kz != 2:
                h_cp[kz].wait_recv()
            block = hbuf[kz]
        normed = (block.astype(f32) * inv * gain[zz * PLANE + p]).astype(bf16)

        def add_c(k, carry):
            term = jnp.dot(normed, wbuf[k, zz], preferred_element_type=f32)
            term_kv = lax.dot_general(
                normed, wkbuf[k, zz], (((1,), (1,)), ((), ())), preferred_element_type=f32
            )
            if kz == 0:
                cpart[k, :, :128] = term
                cpart[k, :, 128:] = term_kv
            else:
                cpart[k, :, :128] = cpart[k, :, :128] + term
                cpart[k, :, 128:] = cpart[k, :, 128:] + term_kv
            return carry

        lax.fori_loop(0, PLANE, add_c, 0)

    rc_cp = {}
    for k in range(1, PLANE):
        rc_cp[k] = remote(cpart.at[k], crecv.at[k], rc_s.at[k], rc_r.at[k], back_chip(k), c)
        rc_cp[k].start()

    grad = dpart[0]
    for k in range(1, PLANE):
        rd_cp[k].wait_recv()
        grad = grad + drecv[k]
    grad = grad.astype(bf16)
    grad_t = lax.dot_general(
        eye, grad, (((1,), (1,)), ((), ())), preferred_element_type=f32
    )
    own_c.wait()

    def wait_c(k, carry):
        c_copy(k).wait()
        return carry

    lax.fori_loop(1, devs, wait_c, 0)
    rows = total_grad.shape[1]
    cache_len = rows * devs
    head_k = cbuf[:, :rows, :].reshape(cache_len, 128)
    head_v = cbuf[:, rows:, :].reshape(cache_len, 128)
    grad_prob = lax.dot_general(
        head_v, grad, (((1,), (1,)), ((), ())), preferred_element_type=f32
    )

    qkv = cpart[0]
    for k in range(1, PLANE):
        rc_cp[k].wait_recv()
        qkv = qkv + crecv[k]
    kv = qkv[:, 128:].astype(bf16)
    kvt[...] = lax.dot_general(
        eye, kv, (((1,), (1,)), ((), ())), preferred_element_type=f32
    ).astype(bf16)

    def kv_part(chip):
        return kvt.at[pl.ds(pl.multiple_of((chip // (chips // KV)) * 16, 16), 16)]

    def kv_copy(k):
        j = (m + k) % chips
        return remote(kv_part(j), kvr.at[m], kv_s.at[k], kv_r.at[k], j, c)

    def start_kv(k, carry):
        kv_copy(k).start()
        return carry

    lax.fori_loop(1, chips, start_kv, 0)
    own_kv = pltpu.make_async_copy(kv_part(m), kvr.at[m], loc.at[2])
    own_kv.start()

    scale = 128 ** (-0.5)
    q_raw = qkv[:, :128]
    turned = jnp.concatenate([q_raw[:, 64:], q_raw[:, :64]], axis=1)
    query = (q_raw * cosd[...] + turned * sind[...]).astype(bf16)
    query_t = lax.dot_general(
        eye, query, (((1,), (1,)), ((), ())), preferred_element_type=f32
    ).astype(bf16)
    score = jnp.dot(head_k, query_t, preferred_element_type=f32) * scale
    top = jnp.max(score, axis=0, keepdims=True)

    def wait_kv(k, carry):
        kv_copy(k).wait()
        return carry

    lax.fori_loop(1, chips, wait_kv, 0)
    own_kv.wait()
    kvf = kvr[...].astype(f32)
    key_t = kvf[:, :8, :].reshape(128, kvf.shape[2])
    value_t = kvf[:, 8:, :].reshape(128, kvf.shape[2]).astype(bf16)
    turned_t = jnp.concatenate([key_t[64:], key_t[:64]], axis=0)
    key_t = (key_t * cos_t + turned_t * sin_t).astype(bf16)
    score_self = (
        lax.dot_general(key_t, query_t, (((0,), (0,)), ((), ())), preferred_element_type=f32)
        * scale
    )
    source = lax.broadcasted_iota(jnp.int32, score_self.shape, 0)
    target = lax.broadcasted_iota(jnp.int32, score_self.shape, 1)
    first, last = jnp.zeros_like(target), lengths[0, 0]
    for n in range(1, lengths.shape[1]):
        first = jnp.where(target >= last, last, first)
        last = last + lengths[0, n]
    allowed = jnp.logical_and(source <= target, source >= first)
    score_self = jnp.where(allowed, score_self, -1e30)
    top = jnp.maximum(top, jnp.max(score_self, axis=0, keepdims=True))
    e_cache = jnp.exp(score - top)
    e_self = jnp.exp(score_self - top)
    inverse = 1.0 / (
        jnp.sum(e_cache, axis=0, keepdims=True) + jnp.sum(e_self, axis=0, keepdims=True)
    )
    prob = e_cache * inverse
    weight = prob.astype(bf16)
    weight_self = (e_self * inverse).astype(bf16)
    attended = lax.dot_general(
        head_v, weight, (((0,), (0,)), ((), ())), preferred_element_type=f32
    ) + jnp.dot(value_t, weight_self, preferred_element_type=f32)
    delta = jnp.sum(grad_t * attended, axis=0, keepdims=True)
    grad_score = (prob * (grad_prob - delta)).astype(bf16)
    value_part = jnp.dot(weight, grad, preferred_element_type=f32).astype(bf16)
    key_part = (jnp.dot(grad_score, query, preferred_element_type=f32) * scale).astype(bf16)
    gsend[:, :rows, :] = key_part.reshape(devs, rows, 128)
    gsend[:, rows:, :] = value_part.reshape(devs, rows, 128)

    def g_copy(k):
        j = (i + k) % devs
        return remote(gsend.at[j], grecv.at[i], g_s.at[k], g_r.at[k], j // 2, j % 2)

    def start_g(k, carry):
        g_copy(k).start()
        return carry

    lax.fori_loop(1, devs, start_g, 0)
    own_g = pltpu.make_async_copy(gsend.at[i], grecv.at[i], loc.at[3])
    own_g.start()

    for k in range(1, LINE):
        when(direct(k), o_cp[k].wait_send)
        when(direct(k), h_cp[k].wait_send)

    @pl.when(inner)
    def _():
        relay(obuf, o_s, o_r).wait_send()
        relay(hbuf, h_s, h_r).wait_send()

    for k in range(1, PLANE):
        w_cp[k].wait_send()
        wf_cp[k].wait_send()
        rd_cp[k].wait_send()
        rc_cp[k].wait_send()
        for h in range(pair):
            wo_cp[k, h].wait_send()
            wof_cp[k, h].wait_send()
            wk_cp[k, h].wait_send()
            wkf_cp[k, h].wait_send()

    def wait_g(k, carry):
        g_copy(k).wait()
        return carry

    lax.fori_loop(1, devs, wait_g, 0)
    own_g.wait()

    share = devs // KV
    for g in range(KV):
        got = jnp.sum(grecv[g * share : (g + 1) * share].astype(f32), axis=0)
        cols = slice(g * 128, (g + 1) * 128)
        for which in range(2):
            total_grad[which, :, cols] = got[which * rows : (which + 1) * rows]


def fused_device(
    hidden,
    out_grad,
    norm_gain,
    w_query,
    w_key,
    w_value,
    w_out,
    cache_keys,
    cache_values,
    first_moment,
    second_moment,
    conv_lengths,
    row_offsets,
):
    chips = LINE * PLANE
    devs = 2 * chips
    f32, bf16 = jnp.float32, jnp.bfloat16
    rows, width = hidden.shape
    pos = cache_keys.shape[0]
    cache_len = pos * devs
    head = w_query.shape[1]
    full = w_query.shape[0]
    w_kv = jnp.stack([w_key.transpose(1, 2, 0), w_value.transpose(1, 2, 0)], axis=1)
    w_kv = w_kv.reshape(head, full)
    ckv = jnp.stack(
        [cache_keys.astype(bf16).reshape(pos, KV, head), cache_values.astype(bf16).reshape(pos, KV, head)]
    )
    ckv = ckv.transpose(2, 0, 1, 3).reshape(KV, 2 * pos, head)
    segment, position = row_layout(conv_lengths[0], row_offsets[0], rows, cache_len)
    cos, sin = rope_tables(position, head)
    cosd = jnp.concatenate([cos, cos], axis=1)
    sind = jnp.concatenate([-sin, sin], axis=1)
    vm = pl.BlockSpec(memory_space=pltpu.VMEM)
    smem = pl.BlockSpec(memory_space=pltpu.SMEM)
    hbm = pl.BlockSpec(memory_space=pl.ANY)
    dma = pltpu.SemaphoreType.DMA
    pair = LINE // 2
    gradient = pl.pallas_call(
        fused_kernel,
        out_shape=jax.ShapeDtypeStruct(first_moment.shape, f32),
        in_specs=[vm, vm, vm, hbm, hbm, hbm, vm, vm, vm, smem],
        out_specs=vm,
        scratch_shapes=[
            pltpu.VMEM((LINE, rows, width), bf16),
            pltpu.VMEM((LINE, rows, width), bf16),
            pltpu.VMEM((8, rows), f32),
            pltpu.VMEM((chips, 8, rows), f32),
            pltpu.VMEM((PLANE, LINE, width, head), bf16),
            pltpu.VMEM((PLANE, LINE, head, width), bf16),
            pltpu.VMEM((PLANE, LINE, head, width), bf16),
            pltpu.VMEM((devs, 2 * pos, head), bf16),
            pltpu.VMEM((PLANE, rows, 2 * head), f32),
            pltpu.VMEM((PLANE, rows, 2 * head), f32),
            pltpu.VMEM((PLANE, rows, head), f32),
            pltpu.VMEM((PLANE, rows, head), f32),
            pltpu.VMEM((head, rows), bf16),
            pltpu.VMEM((chips, 16, rows), bf16),
            pltpu.VMEM((devs, 2 * pos, head), bf16),
            pltpu.VMEM((devs, 2 * pos, head), bf16),
            dma((LINE,)),
            dma((LINE,)),
            dma((LINE,)),
            dma((LINE,)),
            dma((chips,)),
            dma((chips,)),
            dma((PLANE,)),
            dma((PLANE,)),
            dma((PLANE,)),
            dma((PLANE,)),
            dma((PLANE, pair)),
            dma((PLANE, pair)),
            dma((PLANE, pair)),
            dma((PLANE, pair)),
            dma((PLANE, pair)),
            dma((PLANE, pair)),
            dma((PLANE, pair)),
            dma((PLANE, pair)),
            dma((devs,)),
            dma((devs,)),
            dma((PLANE,)),
            dma((PLANE,)),
            dma((PLANE,)),
            dma((PLANE,)),
            dma((chips,)),
            dma((chips,)),
            dma((devs,)),
            dma((devs,)),
            dma((4,)),
            dma((2 * LINE,)),
        ],
        compiler_params=pltpu.CompilerParams(
            collective_id=0, has_side_effects=True, vmem_limit_bytes=56 * 1024 * 1024
        ),
    )(
        hidden,
        out_grad,
        norm_gain.reshape(chips, 1, width),
        w_query.reshape(LINE, PLANE, width, head),
        w_kv,
        w_out,
        ckv,
        cosd,
        sind,
        conv_lengths,
    )
    new_keys, first_k, second_k = adam_update(
        cache_keys, gradient[0], first_moment[0], second_moment[0]
    )
    new_values, first_v, second_v = adam_update(
        cache_values, gradient[1], first_moment[1], second_moment[1]
    )
    return (new_keys, new_values, jnp.stack([first_k, first_v]), jnp.stack([second_k, second_v]))


def solution(mesh):
    return jax.shard_map(
        fused_device if fits(mesh) else per_device,
        mesh=mesh,
        in_specs=(
            P(("groups", "dp"), "cache"),
            P(("groups", "dp"), "cache"),
            P(),
            P(None, "cache"),
            P(None, None, "cache"),
            P(None, None, "cache"),
            P("cache", None),
            P(("groups", "cache", "dp"), None),
            P(("groups", "cache", "dp"), None),
            P(None, ("groups", "cache", "dp"), None),
            P(None, ("groups", "cache", "dp"), None),
            P(("groups", "dp"), None),
            P(("groups", "dp"), None),
        ),
        out_specs=(
            P(("groups", "cache", "dp"), None),
            P(("groups", "cache", "dp"), None),
            P(None, ("groups", "cache", "dp"), None),
            P(None, ("groups", "cache", "dp"), None),
        ),
        check_vma=False,
    )
```

```python
import math

import jax
import jax.numpy as jnp
from jax import lax
from jax.experimental import pallas as pl
from jax.experimental.pallas import tpu as pltpu
from jax.sharding import PartitionSpec as P

KV = 8
ADAM_STEP = 10


THETA = 500000.0
BETA_ONE = 0.9
BETA_TWO = 0.999
RATE = 0.02
EPSILON = 1e-08


def rope_tables(position, head_width):
    half_width = head_width // 2
    inverse = jnp.exp(
        jnp.arange(half_width, dtype=jnp.float32) * (-2.0 * math.log(THETA) / head_width)
    )
    angles = position.astype(jnp.float32)[:, None] * inverse[None, :]
    return (jnp.cos(angles), jnp.sin(angles))


def rotate(tensor, cos_table, sin_table):
    half_width = tensor.shape[1] // 2
    first_half = tensor[:, :half_width]
    second_half = tensor[:, half_width:]
    return jnp.concatenate(
        [
            first_half * cos_table - second_half * sin_table,
            second_half * cos_table + first_half * sin_table,
        ],
        axis=1,
    )


def row_layout(lengths, offsets, row_count, cache_len):
    end_rows = jnp.cumsum(lengths)
    start_rows = end_rows - lengths
    row_index = jnp.arange(row_count, dtype=jnp.int32)
    segment = jnp.sum((row_index[:, None] >= end_rows[None, :]).astype(jnp.int32), axis=1)
    onehot = segment[:, None] == jnp.arange(lengths.shape[0], dtype=jnp.int32)[None, :]
    first_row = jnp.sum(jnp.where(onehot, start_rows[None, :], 0), axis=1)
    offset_row = jnp.sum(jnp.where(onehot, offsets[None, :], 0), axis=1)
    return (segment, cache_len + offset_row + row_index - first_row)


def attend(query, grad_out, cache_k, cache_v, self_k, self_v, allowed, score_scale):
    contract = (((1,), (1,)), ((), ()))
    score_cache = (
        lax.dot_general(query, cache_k, contract, preferred_element_type=jnp.float32) * score_scale
    )
    score_self = (
        lax.dot_general(query, self_k, contract, preferred_element_type=jnp.float32) * score_scale
    )
    score_self = jnp.where(allowed, score_self, -1e30)
    highest = jnp.maximum(
        jnp.max(score_cache, axis=1, keepdims=True), jnp.max(score_self, axis=1, keepdims=True)
    )
    exp_cache = jnp.exp(score_cache - highest)
    exp_self = jnp.exp(score_self - highest)
    denominator = jnp.sum(exp_cache, axis=1, keepdims=True) + jnp.sum(
        exp_self, axis=1, keepdims=True
    )
    prob_cache = exp_cache / denominator
    prob_self = exp_self / denominator
    weight_cache = prob_cache.astype(jnp.bfloat16)
    weight_self = prob_self.astype(jnp.bfloat16)
    attended = jnp.dot(weight_cache, cache_v, preferred_element_type=jnp.float32) + jnp.dot(
        weight_self, self_v, preferred_element_type=jnp.float32
    )
    delta_row = jnp.sum(grad_out.astype(jnp.float32) * attended, axis=1, keepdims=True)
    grad_prob = lax.dot_general(grad_out, cache_v, contract, preferred_element_type=jnp.float32)
    grad_score = (prob_cache * (grad_prob - delta_row)).astype(jnp.bfloat16)
    return (grad_score, weight_cache)


def adam_update(master, gradient, first, second):
    first_new = BETA_ONE * first + (1.0 - BETA_ONE) * gradient
    second_new = BETA_TWO * second + (1.0 - BETA_TWO) * gradient * gradient
    first_hat = first_new / (1.0 - BETA_ONE**ADAM_STEP)
    second_hat = second_new / (1.0 - BETA_TWO**ADAM_STEP)
    return (master - RATE * first_hat / (jnp.sqrt(second_hat) + EPSILON), first_new, second_new)


def source_total(pieces):
    head_width = pieces.shape[2]
    item_count = pieces.shape[1]
    summed = (
        pieces.astype(jnp.float32)
        .reshape(KV, pieces.shape[0] // KV, item_count, head_width)
        .sum(axis=1)
    )
    return summed.transpose(1, 0, 2).reshape(item_count, KV * head_width)


def totals_pair(pieces):
    return (source_total(pieces[0]), source_total(pieces[1]))


def per_device(
    hidden,
    out_grad,
    norm_gain,
    w_query,
    w_key,
    w_value,
    w_out,
    cache_keys,
    cache_values,
    first_moment,
    second_moment,
    conv_lengths,
    row_offsets,
):
    cache_count = lax.axis_size("cache")
    data_count = lax.axis_size("dp")
    pos_count = cache_keys.shape[0]
    device_count = cache_count * data_count
    cache_len = pos_count * device_count
    head_width = w_query.shape[1]
    column_share = w_key.shape[2]
    groups = cache_count // KV
    kv_head = lax.axis_index("cache") // groups
    score_scale = head_width ** (-0.5)
    hidden_full, grad_full = (
        lax.all_gather(hidden, "cache", axis=1, tiled=True),
        lax.all_gather(out_grad, "cache", axis=1, tiled=True),
    )
    row_count = hidden_full.shape[0]
    width_full = hidden_full.shape[1]
    hidden_f = hidden_full.astype(jnp.float32)
    inv_rms = lax.rsqrt(jnp.mean(hidden_f * hidden_f, axis=1, keepdims=True) + 1e-05)
    normed = (hidden_f * inv_rms * norm_gain).astype(jnp.bfloat16)
    segment, position = row_layout(conv_lengths[0], row_offsets[0], row_count, cache_len)
    cos_table, sin_table = rope_tables(position, head_width)
    query = rotate(
        jnp.dot(normed, w_query, preferred_element_type=jnp.float32), cos_table, sin_table
    ).astype(jnp.bfloat16)
    key_piece = (
        jnp.dot(
            normed, w_key.reshape(width_full, KV * column_share), preferred_element_type=jnp.float32
        )
        .astype(jnp.bfloat16)
        .reshape(row_count, KV, column_share)
    )
    value_piece = (
        jnp.dot(
            normed,
            w_value.reshape(width_full, KV * column_share),
            preferred_element_type=jnp.float32,
        )
        .astype(jnp.bfloat16)
        .reshape(row_count, KV, column_share)
    )
    keys_raw, values_self = (
        lax.all_gather(key_piece, "cache", axis=2, tiled=True),
        lax.all_gather(value_piece, "cache", axis=2, tiled=True),
    )
    own_keys = lax.dynamic_slice_in_dim(keys_raw, kv_head, 1, 1).reshape(row_count, head_width)
    self_k = rotate(own_keys.astype(jnp.float32), cos_table, sin_table).astype(jnp.bfloat16)
    self_v = lax.dynamic_slice_in_dim(values_self, kv_head, 1, 1).reshape(row_count, head_width)
    grad_out = lax.dot_general(
        grad_full, w_out, (((1,), (1,)), ((), ())), preferred_element_type=jnp.float32
    ).astype(jnp.bfloat16)
    cache_k = cache_keys.astype(jnp.bfloat16)
    cache_v = cache_values.astype(jnp.bfloat16)
    keys_all, values_all = (
        lax.all_gather(cache_k, ("cache", "dp"), axis=0, tiled=True),
        lax.all_gather(cache_v, ("cache", "dp"), axis=0, tiled=True),
    )
    head_k = lax.dynamic_slice_in_dim(keys_all, kv_head * head_width, head_width, 1)
    head_v = lax.dynamic_slice_in_dim(values_all, kv_head * head_width, head_width, 1)
    row_index = jnp.arange(row_count, dtype=jnp.int32)
    allowed = (segment[:, None] == segment[None, :]) & (row_index[None, :] <= row_index[:, None])
    grad_score, weight_cache = attend(
        query, grad_out, head_k, head_v, self_k, self_v, allowed, score_scale
    )
    transposed = (((0,), (0,)), ((), ()))
    key_part = (
        lax.dot_general(grad_score, query, transposed, preferred_element_type=jnp.float32)
        * score_scale
    ).astype(jnp.bfloat16)
    value_part = lax.dot_general(
        weight_cache, grad_out, transposed, preferred_element_type=jnp.float32
    ).astype(jnp.bfloat16)
    send_k = key_part.reshape(device_count, pos_count, head_width)
    send_v = value_part.reshape(device_count, pos_count, head_width)
    grad_k, grad_v = totals_pair(
        (
            lax.all_to_all(send_k, ("cache", "dp"), split_axis=0, concat_axis=0, tiled=True),
            lax.all_to_all(send_v, ("cache", "dp"), split_axis=0, concat_axis=0, tiled=True),
        )
    )
    gradient = jnp.stack([grad_k, grad_v])
    master = jnp.stack([cache_keys, cache_values])
    new_master, first_new, second_new = adam_update(master, gradient, first_moment, second_moment)
    return (new_master[0], new_master[1], first_new, second_new)


LINE = 4
PLANE = 4
MESH = pl.DeviceIdType.MESH


def fits(mesh):
    return mesh.shape["cache"] == LINE * PLANE and mesh.shape["dp"] == 2


def fused_kernel(
    hid,
    og,
    gain,
    wq,
    wkv,
    wout,
    ckv,
    cosd,
    sind,
    lengths,
    total_grad,
    hbuf,
    obuf,
    ss_in,
    srecv,
    wbuf,
    wkbuf,
    wobuf,
    cbuf,
    cpart,
    crecv,
    dpart,
    drecv,
    kvt,
    kvr,
    gsend,
    grecv,
    h_s,
    h_r,
    o_s,
    o_r,
    s_s,
    s_r,
    w_s,
    w_r,
    wf_s,
    wf_r,
    wk_s,
    wk_r,
    wkf_s,
    wkf_r,
    wo_s,
    wo_r,
    wof_s,
    wof_r,
    c_s,
    c_r,
    rc_s,
    rc_r,
    rd_s,
    rd_r,
    kv_s,
    kv_r,
    g_s,
    g_r,
    loc,
    loco,
):
    chips = LINE * PLANE
    devs = 2 * chips
    m = lax.axis_index("cache")
    c = lax.axis_index("dp")
    i = m * 2 + c
    line, p = m // PLANE, m % PLANE
    width = hid.shape[1]
    pair = LINE // 2
    mine = c * pair
    other = (1 - c) * pair
    f32, bf16 = jnp.float32, jnp.bfloat16

    barrier = pltpu.get_barrier_semaphore()

    def greet(k, carry):
        j = (i + k) % devs
        pl.semaphore_signal(
            barrier, inc=1, device_id={"cache": j // 2, "dp": j % 2}, device_id_type=MESH
        )
        return carry

    lax.fori_loop(1, devs, greet, 0)

    own_w = pltpu.make_async_copy(wq.at[:, p], wbuf.at[0], loc.at[0])
    own_w.start()
    own_wo = []
    for zz in range(LINE):
        col = pl.multiple_of((zz * PLANE + p) * width, width)
        cp = pltpu.make_async_copy(wout.at[:, pl.ds(col, width)], wobuf.at[0, zz], loco.at[zz])
        cp.start()
        own_wo.append(cp)
        cp = pltpu.make_async_copy(
            wkv.at[:, pl.ds(col, width)], wkbuf.at[0, zz], loco.at[LINE + zz]
        )
        cp.start()
        own_wo.append(cp)
    own_c = pltpu.make_async_copy(ckv.at[m // (chips // KV)], cbuf.at[i], loc.at[1])
    own_c.start()
    own_f = hid[...].astype(f32)
    ss_in[...] = lax.dot_general(
        jnp.ones((8, width), f32),
        own_f * own_f,
        (((1,), (1,)), ((), ())),
        preferred_element_type=f32,
        precision=lax.Precision.HIGHEST,
    )
    pl.semaphore_wait(barrier, devs - 1)

    def remote(src, dst, ss, rs, chip, core):
        return pltpu.make_async_remote_copy(
            src_ref=src,
            dst_ref=dst,
            send_sem=ss,
            recv_sem=rs,
            device_id={"cache": chip, "dp": core},
            device_id_type=MESH,
        )

    def ss_copy(k):
        return remote(ss_in, srecv.at[k], s_s.at[k], s_r.at[k], (m + k) % chips, c)

    def start_ss(k, carry):
        ss_copy(k).start()
        return carry

    lax.fori_loop(1, chips, start_ss, 0)

    def line_chip(k):
        return ((line + k) % LINE) * PLANE + p

    def plane_chip(k):
        return line * PLANE + (p + k) % PLANE

    def back_chip(k):
        return line * PLANE + (p + PLANE - k) % PLANE

    inner = jnp.logical_and(line > 0, line < LINE - 1)

    def direct(k):
        if k == LINE - 1:
            return line != 0
        if k == 1:
            return line != LINE - 1
        return None

    def when(cond, act):
        if cond is None:
            act()
        else:
            pl.when(cond)(act)

    def relay(buf, ss, rs):
        slot = 2 * line - 1
        return remote(
            buf.at[2], buf.at[slot], ss.at[0], rs.at[slot], 3 * (line - 1) * PLANE + p, c
        )

    o_cp, h_cp, w_cp, wo_cp, wk_cp = {}, {}, {}, {}, {}
    for k in (2, 1, 3):
        o_cp[k] = remote(og, obuf.at[k], o_s.at[k], o_r.at[k], line_chip(k), c)
        when(direct(k), o_cp[k].start)

    def send_rows(src, buf, ss, rs, cps):
        for k in range(1, PLANE):
            for h in range(pair):
                col = pl.multiple_of(((mine + h) * PLANE + (p + k) % PLANE) * width, width)
                cps[k, h] = remote(
                    src.at[:, pl.ds(col, width)],
                    buf.at[k, mine + h],
                    ss.at[k, h],
                    rs.at[k, h],
                    plane_chip(k),
                    c,
                )
                cps[k, h].start()

    send_rows(wout, wobuf, wo_s, wo_r, wo_cp)
    for k in (2, 1, 3):
        h_cp[k] = remote(hid, hbuf.at[k], h_s.at[k], h_r.at[k], line_chip(k), c)
        when(direct(k), h_cp[k].start)
    for k in range(1, PLANE):
        w_cp[k] = remote(
            wq.at[pl.ds(mine, pair), (p + k) % PLANE],
            wbuf.at[k, pl.ds(mine, pair)],
            w_s.at[k],
            w_r.at[k],
            plane_chip(k),
            c,
        )
        w_cp[k].start()
    send_rows(wkv, wkbuf, wk_s, wk_r, wk_cp)

    def c_copy(k):
        j = (i + k) % devs
        return remote(
            ckv.at[(j // 2) // (chips // KV)], cbuf.at[i], c_s.at[k], c_r.at[k], j // 2, j % 2
        )

    def start_c(k, carry):
        c_copy(k).start()
        return carry

    lax.fori_loop(1, devs, start_c, 0)

    o_cp[2].wait_recv()

    @pl.when(inner)
    def _():
        relay(obuf, o_s, o_r).start()

    wof_cp = {}
    for k in range(1, PLANE):
        for h in range(pair):
            wo_cp[k, h].wait_recv()
            wof_cp[k, h] = remote(
                wobuf.at[k, mine + h],
                wobuf.at[k, mine + h],
                wof_s.at[k, h],
                wof_r.at[k, h],
                m,
                1 - c,
            )
            wof_cp[k, h].start()

    @pl.when(inner)
    def _():
        h_cp[2].wait_recv()
        relay(hbuf, h_s, h_r).start()

    for cp in own_wo:
        cp.wait()
    for k in range(1, PLANE):
        for h in range(pair):
            wof_cp[k, h].wait_recv()

    for kz in range(LINE):
        if kz == 0:
            block = og[...]
        else:
            if kz != 2:
                o_cp[kz].wait_recv()
            block = obuf[kz]
        zz = (line + LINE - kz) % LINE

        def add_d(k, carry):
            term = lax.dot_general(
                block, wobuf[k, zz], (((1,), (1,)), ((), ())), preferred_element_type=f32
            )
            if kz == 0:
                dpart[k] = term
            else:
                dpart[k] = dpart[k] + term
            return carry

        lax.fori_loop(0, PLANE, add_d, 0)

    rd_cp = {}
    for k in range(1, PLANE):
        rd_cp[k] = remote(dpart.at[k], drecv.at[k], rd_s.at[k], rd_r.at[k], back_chip(k), c)
        rd_cp[k].start()

    pl.when(jnp.logical_not(inner))(h_cp[2].wait_recv)
    wf_cp, wkf_cp = {}, {}
    for k in range(1, PLANE):
        w_cp[k].wait_recv()
        part = wbuf.at[k, pl.ds(mine, pair)]
        wf_cp[k] = remote(part, part, wf_s.at[k], wf_r.at[k], m, 1 - c)
        wf_cp[k].start()
        for h in range(pair):
            wk_cp[k, h].wait_recv()
            part = wkbuf.at[k, mine + h]
            wkf_cp[k, h] = remote(part, part, wkf_s.at[k, h], wkf_r.at[k, h], m, 1 - c)
            wkf_cp[k, h].start()

    unit = (
        lax.broadcasted_iota(jnp.int32, (128, 128), 0)
        == lax.broadcasted_iota(jnp.int32, (128, 128), 1)
    ).astype(f32)
    eye = unit.astype(bf16)

    def flip(table):
        return lax.dot_general(
            unit,
            table,
            (((1,), (1,)), ((), ())),
            preferred_element_type=f32,
            precision=lax.Precision.HIGHEST,
        )

    cos_t, sin_t = flip(cosd[...]), flip(sind[...])

    def wait_ss(k, carry):
        ss_copy(k).wait()
        return carry

    lax.fori_loop(1, chips, wait_ss, 0)
    srecv[0] = ss_in[...]
    total = jnp.sum(srecv[...], axis=0)
    spread = lax.dot_general(
        total,
        jnp.full((8, 128), 0.125, f32),
        (((0,), (0,)), ((), ())),
        preferred_element_type=f32,
        precision=lax.Precision.HIGHEST,
    )
    inv = lax.rsqrt(spread[:, :1] * (1.0 / (width * chips)) + 1e-05)
    own_w.wait()
    for k in range(1, PLANE):
        wf_cp[k].wait_recv()
        for h in range(pair):
            wkf_cp[k, h].wait_recv()
    for kz in range(LINE):
        zz = (line + LINE - kz) % LINE
        if kz == 0:
            block = hid[...]
        else:
            if kz != 2:
                h_cp[kz].wait_recv()
            block = hbuf[kz]
        normed = (block.astype(f32) * inv * gain[zz * PLANE + p]).astype(bf16)

        def add_c(k, carry):
            term = jnp.dot(normed, wbuf[k, zz], preferred_element_type=f32)
            term_kv = lax.dot_general(
                normed, wkbuf[k, zz], (((1,), (1,)), ((), ())), preferred_element_type=f32
            )
            if kz == 0:
                cpart[k, :, :128] = term
                cpart[k, :, 128:] = term_kv
            else:
                cpart[k, :, :128] = cpart[k, :, :128] + term
                cpart[k, :, 128:] = cpart[k, :, 128:] + term_kv
            return carry

        lax.fori_loop(0, PLANE, add_c, 0)

    rc_cp = {}
    for k in range(1, PLANE):
        rc_cp[k] = remote(cpart.at[k], crecv.at[k], rc_s.at[k], rc_r.at[k], back_chip(k), c)
        rc_cp[k].start()

    grad = dpart[0]
    for k in range(1, PLANE):
        rd_cp[k].wait_recv()
        grad = grad + drecv[k]
    grad = grad.astype(bf16)
    grad_t = lax.dot_general(
        eye, grad, (((1,), (1,)), ((), ())), preferred_element_type=f32
    )
    own_c.wait()

    def wait_c(k, carry):
        c_copy(k).wait()
        return carry

    lax.fori_loop(1, devs, wait_c, 0)
    rows = total_grad.shape[1]
    cache_len = rows * devs
    head_k = cbuf[:, :rows, :].reshape(cache_len, 128)
    head_v = cbuf[:, rows:, :].reshape(cache_len, 128)
    grad_prob = lax.dot_general(
        head_v, grad, (((1,), (1,)), ((), ())), preferred_element_type=f32
    )

    qkv = cpart[0]
    for k in range(1, PLANE):
        rc_cp[k].wait_recv()
        qkv = qkv + crecv[k]
    kv = qkv[:, 128:].astype(bf16)
    kvt[...] = lax.dot_general(
        eye, kv, (((1,), (1,)), ((), ())), preferred_element_type=f32
    ).astype(bf16)

    def kv_part(chip):
        return kvt.at[pl.ds(pl.multiple_of((chip // (chips // KV)) * 16, 16), 16)]

    def kv_copy(k):
        j = (m + k) % chips
        return remote(kv_part(j), kvr.at[m], kv_s.at[k], kv_r.at[k], j, c)

    def start_kv(k, carry):
        kv_copy(k).start()
        return carry

    lax.fori_loop(1, chips, start_kv, 0)
    own_kv = pltpu.make_async_copy(kv_part(m), kvr.at[m], loc.at[2])
    own_kv.start()

    scale = 128 ** (-0.5)
    q_raw = qkv[:, :128]
    turned = jnp.concatenate([q_raw[:, 64:], q_raw[:, :64]], axis=1)
    query = (q_raw * cosd[...] + turned * sind[...]).astype(bf16)
    query_t = lax.dot_general(
        eye, query, (((1,), (1,)), ((), ())), preferred_element_type=f32
    ).astype(bf16)
    score = jnp.dot(head_k, query_t, preferred_element_type=f32) * scale
    top = jnp.max(score, axis=0, keepdims=True)

    def wait_kv(k, carry):
        kv_copy(k).wait()
        return carry

    lax.fori_loop(1, chips, wait_kv, 0)
    own_kv.wait()
    kvf = kvr[...].astype(f32)
    key_t = kvf[:, :8, :].reshape(128, kvf.shape[2])
    value_t = kvf[:, 8:, :].reshape(128, kvf.shape[2]).astype(bf16)
    turned_t = jnp.concatenate([key_t[64:], key_t[:64]], axis=0)
    key_t = (key_t * cos_t + turned_t * sin_t).astype(bf16)
    score_self = (
        lax.dot_general(key_t, query_t, (((0,), (0,)), ((), ())), preferred_element_type=f32)
        * scale
    )
    source = lax.broadcasted_iota(jnp.int32, score_self.shape, 0)
    target = lax.broadcasted_iota(jnp.int32, score_self.shape, 1)
    first, last = jnp.zeros_like(target), lengths[0, 0]
    for n in range(1, lengths.shape[1]):
        first = jnp.where(target >= last, last, first)
        last = last + lengths[0, n]
    allowed = jnp.logical_and(source <= target, source >= first)
    score_self = jnp.where(allowed, score_self, -1e30)
    top = jnp.maximum(top, jnp.max(score_self, axis=0, keepdims=True))
    e_cache = jnp.exp(score - top)
    e_self = jnp.exp(score_self - top)
    inverse = 1.0 / (
        jnp.sum(e_cache, axis=0, keepdims=True) + jnp.sum(e_self, axis=0, keepdims=True)
    )
    prob = e_cache * inverse
    weight = prob.astype(bf16)
    weight_self = (e_self * inverse).astype(bf16)
    value_part = jnp.dot(weight, grad, preferred_element_type=f32).astype(bf16)
    gsend[:, rows:, :] = value_part.reshape(devs, rows, 128)

    def g_copy(k, which):
        j = (i + k) % devs
        part = pl.ds(which * rows, rows)
        return remote(
            gsend.at[j, part], grecv.at[i, part], g_s.at[which, k], g_r.at[which, k], j // 2, j % 2
        )

    def start_g(which):
        def start(k, carry):
            g_copy(k, which).start()
            return carry

        lax.fori_loop(1, devs, start, 0)

    start_g(1)
    attended = lax.dot_general(
        head_v, weight, (((0,), (0,)), ((), ())), preferred_element_type=f32
    ) + jnp.dot(value_t, weight_self, preferred_element_type=f32)
    delta = jnp.sum(grad_t * attended, axis=0, keepdims=True)
    grad_score = (prob * (grad_prob - delta)).astype(bf16)
    key_part = (jnp.dot(grad_score, query, preferred_element_type=f32) * scale).astype(bf16)
    gsend[:, :rows, :] = key_part.reshape(devs, rows, 128)
    start_g(0)
    own_g = pltpu.make_async_copy(gsend.at[i], grecv.at[i], loc.at[3])
    own_g.start()

    for k in range(1, LINE):
        when(direct(k), o_cp[k].wait_send)
        when(direct(k), h_cp[k].wait_send)

    @pl.when(inner)
    def _():
        relay(obuf, o_s, o_r).wait_send()
        relay(hbuf, h_s, h_r).wait_send()

    for k in range(1, PLANE):
        w_cp[k].wait_send()
        wf_cp[k].wait_send()
        rd_cp[k].wait_send()
        rc_cp[k].wait_send()
        for h in range(pair):
            wo_cp[k, h].wait_send()
            wof_cp[k, h].wait_send()
            wk_cp[k, h].wait_send()
            wkf_cp[k, h].wait_send()

    def wait_g(k, carry):
        g_copy(k, 1).wait()
        g_copy(k, 0).wait()
        return carry

    lax.fori_loop(1, devs, wait_g, 0)
    own_g.wait()

    share = devs // KV
    for g in range(KV):
        got = jnp.sum(grecv[g * share : (g + 1) * share].astype(f32), axis=0)
        cols = slice(g * 128, (g + 1) * 128)
        for which in range(2):
            total_grad[which, :, cols] = got[which * rows : (which + 1) * rows]


def fused_device(
    hidden,
    out_grad,
    norm_gain,
    w_query,
    w_key,
    w_value,
    w_out,
    cache_keys,
    cache_values,
    first_moment,
    second_moment,
    conv_lengths,
    row_offsets,
):
    chips = LINE * PLANE
    devs = 2 * chips
    f32, bf16 = jnp.float32, jnp.bfloat16
    rows, width = hidden.shape
    pos = cache_keys.shape[0]
    cache_len = pos * devs
    head = w_query.shape[1]
    full = w_query.shape[0]
    w_kv = jnp.stack([w_key.transpose(1, 2, 0), w_value.transpose(1, 2, 0)], axis=1)
    w_kv = w_kv.reshape(head, full)
    ckv = jnp.stack(
        [cache_keys.astype(bf16).reshape(pos, KV, head), cache_values.astype(bf16).reshape(pos, KV, head)]
    )
    ckv = ckv.transpose(2, 0, 1, 3).reshape(KV, 2 * pos, head)
    segment, position = row_layout(conv_lengths[0], row_offsets[0], rows, cache_len)
    cos, sin = rope_tables(position, head)
    cosd = jnp.concatenate([cos, cos], axis=1)
    sind = jnp.concatenate([-sin, sin], axis=1)
    vm = pl.BlockSpec(memory_space=pltpu.VMEM)
    smem = pl.BlockSpec(memory_space=pltpu.SMEM)
    hbm = pl.BlockSpec(memory_space=pl.ANY)
    dma = pltpu.SemaphoreType.DMA
    pair = LINE // 2
    gradient = pl.pallas_call(
        fused_kernel,
        out_shape=jax.ShapeDtypeStruct(first_moment.shape, f32),
        in_specs=[vm, vm, vm, hbm, hbm, hbm, vm, vm, vm, smem],
        out_specs=vm,
        scratch_shapes=[
            pltpu.VMEM((LINE, rows, width), bf16),
            pltpu.VMEM((LINE, rows, width), bf16),
            pltpu.VMEM((8, rows), f32),
            pltpu.VMEM((chips, 8, rows), f32),
            pltpu.VMEM((PLANE, LINE, width, head), bf16),
            pltpu.VMEM((PLANE, LINE, head, width), bf16),
            pltpu.VMEM((PLANE, LINE, head, width), bf16),
            pltpu.VMEM((devs, 2 * pos, head), bf16),
            pltpu.VMEM((PLANE, rows, 2 * head), f32),
            pltpu.VMEM((PLANE, rows, 2 * head), f32),
            pltpu.VMEM((PLANE, rows, head), f32),
            pltpu.VMEM((PLANE, rows, head), f32),
            pltpu.VMEM((head, rows), bf16),
            pltpu.VMEM((chips, 16, rows), bf16),
            pltpu.VMEM((devs, 2 * pos, head), bf16),
            pltpu.VMEM((devs, 2 * pos, head), bf16),
            dma((LINE,)),
            dma((LINE,)),
            dma((LINE,)),
            dma((LINE,)),
            dma((chips,)),
            dma((chips,)),
            dma((PLANE,)),
            dma((PLANE,)),
            dma((PLANE,)),
            dma((PLANE,)),
            dma((PLANE, pair)),
            dma((PLANE, pair)),
            dma((PLANE, pair)),
            dma((PLANE, pair)),
            dma((PLANE, pair)),
            dma((PLANE, pair)),
            dma((PLANE, pair)),
            dma((PLANE, pair)),
            dma((devs,)),
            dma((devs,)),
            dma((PLANE,)),
            dma((PLANE,)),
            dma((PLANE,)),
            dma((PLANE,)),
            dma((chips,)),
            dma((chips,)),
            dma((2, devs)),
            dma((2, devs)),
            dma((4,)),
            dma((2 * LINE,)),
        ],
        compiler_params=pltpu.CompilerParams(
            collective_id=0, has_side_effects=True, vmem_limit_bytes=56 * 1024 * 1024
        ),
    )(
        hidden,
        out_grad,
        norm_gain.reshape(chips, 1, width),
        w_query.reshape(LINE, PLANE, width, head),
        w_kv,
        w_out,
        ckv,
        cosd,
        sind,
        conv_lengths,
    )
    new_keys, first_k, second_k = adam_update(
        cache_keys, gradient[0], first_moment[0], second_moment[0]
    )
    new_values, first_v, second_v = adam_update(
        cache_values, gradient[1], first_moment[1], second_moment[1]
    )
    return (new_keys, new_values, jnp.stack([first_k, first_v]), jnp.stack([second_k, second_v]))


def solution(mesh):
    return jax.shard_map(
        fused_device if fits(mesh) else per_device,
        mesh=mesh,
        in_specs=(
            P(("groups", "dp"), "cache"),
            P(("groups", "dp"), "cache"),
            P(),
            P(None, "cache"),
            P(None, None, "cache"),
            P(None, None, "cache"),
            P("cache", None),
            P(("groups", "cache", "dp"), None),
            P(("groups", "cache", "dp"), None),
            P(None, ("groups", "cache", "dp"), None),
            P(None, ("groups", "cache", "dp"), None),
            P(("groups", "dp"), None),
            P(("groups", "dp"), None),
        ),
        out_specs=(
            P(("groups", "cache", "dp"), None),
            P(("groups", "cache", "dp"), None),
            P(None, ("groups", "cache", "dp"), None),
            P(None, ("groups", "cache", "dp"), None),
        ),
        check_vma=False,
    )
```

```python
import math

import jax
import jax.numpy as jnp
from jax import lax
from jax.experimental import pallas as pl
from jax.experimental.pallas import tpu as pltpu
from jax.sharding import PartitionSpec as P

KV = 8
ADAM_STEP = 10


THETA = 500000.0
BETA_ONE = 0.9
BETA_TWO = 0.999
RATE = 0.02
EPSILON = 1e-08


def rope_tables(position, head_width):
    half_width = head_width // 2
    inverse = jnp.exp(
        jnp.arange(half_width, dtype=jnp.float32) * (-2.0 * math.log(THETA) / head_width)
    )
    angles = position.astype(jnp.float32)[:, None] * inverse[None, :]
    return (jnp.cos(angles), jnp.sin(angles))


def rotate(tensor, cos_table, sin_table):
    half_width = tensor.shape[1] // 2
    first_half = tensor[:, :half_width]
    second_half = tensor[:, half_width:]
    return jnp.concatenate(
        [
            first_half * cos_table - second_half * sin_table,
            second_half * cos_table + first_half * sin_table,
        ],
        axis=1,
    )


def row_layout(lengths, offsets, row_count, cache_len):
    end_rows = jnp.cumsum(lengths)
    start_rows = end_rows - lengths
    row_index = jnp.arange(row_count, dtype=jnp.int32)
    segment = jnp.sum((row_index[:, None] >= end_rows[None, :]).astype(jnp.int32), axis=1)
    onehot = segment[:, None] == jnp.arange(lengths.shape[0], dtype=jnp.int32)[None, :]
    first_row = jnp.sum(jnp.where(onehot, start_rows[None, :], 0), axis=1)
    offset_row = jnp.sum(jnp.where(onehot, offsets[None, :], 0), axis=1)
    return (segment, cache_len + offset_row + row_index - first_row)


def attend(query, grad_out, cache_k, cache_v, self_k, self_v, allowed, score_scale):
    contract = (((1,), (1,)), ((), ()))
    score_cache = (
        lax.dot_general(query, cache_k, contract, preferred_element_type=jnp.float32) * score_scale
    )
    score_self = (
        lax.dot_general(query, self_k, contract, preferred_element_type=jnp.float32) * score_scale
    )
    score_self = jnp.where(allowed, score_self, -1e30)
    highest = jnp.maximum(
        jnp.max(score_cache, axis=1, keepdims=True), jnp.max(score_self, axis=1, keepdims=True)
    )
    exp_cache = jnp.exp(score_cache - highest)
    exp_self = jnp.exp(score_self - highest)
    denominator = jnp.sum(exp_cache, axis=1, keepdims=True) + jnp.sum(
        exp_self, axis=1, keepdims=True
    )
    prob_cache = exp_cache / denominator
    prob_self = exp_self / denominator
    weight_cache = prob_cache.astype(jnp.bfloat16)
    weight_self = prob_self.astype(jnp.bfloat16)
    attended = jnp.dot(weight_cache, cache_v, preferred_element_type=jnp.float32) + jnp.dot(
        weight_self, self_v, preferred_element_type=jnp.float32
    )
    delta_row = jnp.sum(grad_out.astype(jnp.float32) * attended, axis=1, keepdims=True)
    grad_prob = lax.dot_general(grad_out, cache_v, contract, preferred_element_type=jnp.float32)
    grad_score = (prob_cache * (grad_prob - delta_row)).astype(jnp.bfloat16)
    return (grad_score, weight_cache)


def adam_update(master, gradient, first, second):
    first_new = BETA_ONE * first + (1.0 - BETA_ONE) * gradient
    second_new = BETA_TWO * second + (1.0 - BETA_TWO) * gradient * gradient
    first_hat = first_new / (1.0 - BETA_ONE**ADAM_STEP)
    second_hat = second_new / (1.0 - BETA_TWO**ADAM_STEP)
    return (master - RATE * first_hat / (jnp.sqrt(second_hat) + EPSILON), first_new, second_new)


def source_total(pieces):
    head_width = pieces.shape[2]
    item_count = pieces.shape[1]
    summed = (
        pieces.astype(jnp.float32)
        .reshape(KV, pieces.shape[0] // KV, item_count, head_width)
        .sum(axis=1)
    )
    return summed.transpose(1, 0, 2).reshape(item_count, KV * head_width)


def totals_pair(pieces):
    return (source_total(pieces[0]), source_total(pieces[1]))


def per_device(
    hidden,
    out_grad,
    norm_gain,
    w_query,
    w_key,
    w_value,
    w_out,
    cache_keys,
    cache_values,
    first_moment,
    second_moment,
    conv_lengths,
    row_offsets,
):
    cache_count = lax.axis_size("cache")
    data_count = lax.axis_size("dp")
    pos_count = cache_keys.shape[0]
    device_count = cache_count * data_count
    cache_len = pos_count * device_count
    head_width = w_query.shape[1]
    column_share = w_key.shape[2]
    groups = cache_count // KV
    kv_head = lax.axis_index("cache") // groups
    score_scale = head_width ** (-0.5)
    hidden_full, grad_full = (
        lax.all_gather(hidden, "cache", axis=1, tiled=True),
        lax.all_gather(out_grad, "cache", axis=1, tiled=True),
    )
    row_count = hidden_full.shape[0]
    width_full = hidden_full.shape[1]
    hidden_f = hidden_full.astype(jnp.float32)
    inv_rms = lax.rsqrt(jnp.mean(hidden_f * hidden_f, axis=1, keepdims=True) + 1e-05)
    normed = (hidden_f * inv_rms * norm_gain).astype(jnp.bfloat16)
    segment, position = row_layout(conv_lengths[0], row_offsets[0], row_count, cache_len)
    cos_table, sin_table = rope_tables(position, head_width)
    query = rotate(
        jnp.dot(normed, w_query, preferred_element_type=jnp.float32), cos_table, sin_table
    ).astype(jnp.bfloat16)
    key_piece = (
        jnp.dot(
            normed, w_key.reshape(width_full, KV * column_share), preferred_element_type=jnp.float32
        )
        .astype(jnp.bfloat16)
        .reshape(row_count, KV, column_share)
    )
    value_piece = (
        jnp.dot(
            normed,
            w_value.reshape(width_full, KV * column_share),
            preferred_element_type=jnp.float32,
        )
        .astype(jnp.bfloat16)
        .reshape(row_count, KV, column_share)
    )
    keys_raw, values_self = (
        lax.all_gather(key_piece, "cache", axis=2, tiled=True),
        lax.all_gather(value_piece, "cache", axis=2, tiled=True),
    )
    own_keys = lax.dynamic_slice_in_dim(keys_raw, kv_head, 1, 1).reshape(row_count, head_width)
    self_k = rotate(own_keys.astype(jnp.float32), cos_table, sin_table).astype(jnp.bfloat16)
    self_v = lax.dynamic_slice_in_dim(values_self, kv_head, 1, 1).reshape(row_count, head_width)
    grad_out = lax.dot_general(
        grad_full, w_out, (((1,), (1,)), ((), ())), preferred_element_type=jnp.float32
    ).astype(jnp.bfloat16)
    cache_k = cache_keys.astype(jnp.bfloat16)
    cache_v = cache_values.astype(jnp.bfloat16)
    keys_all, values_all = (
        lax.all_gather(cache_k, ("cache", "dp"), axis=0, tiled=True),
        lax.all_gather(cache_v, ("cache", "dp"), axis=0, tiled=True),
    )
    head_k = lax.dynamic_slice_in_dim(keys_all, kv_head * head_width, head_width, 1)
    head_v = lax.dynamic_slice_in_dim(values_all, kv_head * head_width, head_width, 1)
    row_index = jnp.arange(row_count, dtype=jnp.int32)
    allowed = (segment[:, None] == segment[None, :]) & (row_index[None, :] <= row_index[:, None])
    grad_score, weight_cache = attend(
        query, grad_out, head_k, head_v, self_k, self_v, allowed, score_scale
    )
    transposed = (((0,), (0,)), ((), ()))
    key_part = (
        lax.dot_general(grad_score, query, transposed, preferred_element_type=jnp.float32)
        * score_scale
    ).astype(jnp.bfloat16)
    value_part = lax.dot_general(
        weight_cache, grad_out, transposed, preferred_element_type=jnp.float32
    ).astype(jnp.bfloat16)
    send_k = key_part.reshape(device_count, pos_count, head_width)
    send_v = value_part.reshape(device_count, pos_count, head_width)
    grad_k, grad_v = totals_pair(
        (
            lax.all_to_all(send_k, ("cache", "dp"), split_axis=0, concat_axis=0, tiled=True),
            lax.all_to_all(send_v, ("cache", "dp"), split_axis=0, concat_axis=0, tiled=True),
        )
    )
    gradient = jnp.stack([grad_k, grad_v])
    master = jnp.stack([cache_keys, cache_values])
    new_master, first_new, second_new = adam_update(master, gradient, first_moment, second_moment)
    return (new_master[0], new_master[1], first_new, second_new)


LINE = 4
PLANE = 4
MESH = pl.DeviceIdType.MESH


def fits(mesh):
    return mesh.shape["cache"] == LINE * PLANE and mesh.shape["dp"] == 2


def fused_kernel(
    hid,
    og,
    gain,
    wq,
    wkv,
    wout,
    ckv,
    cosd,
    sind,
    lengths,
    total_grad,
    hbuf,
    obuf,
    ss_in,
    srecv,
    wbuf,
    wkbuf,
    wobuf,
    cbuf,
    cpart,
    crecv,
    dpart,
    drecv,
    kvt,
    kvr,
    gsend,
    grecv,
    h_s,
    h_r,
    o_s,
    o_r,
    s_s,
    s_r,
    w_s,
    w_r,
    wf_s,
    wf_r,
    wk_s,
    wk_r,
    wkf_s,
    wkf_r,
    wo_s,
    wo_r,
    wof_s,
    wof_r,
    c_s,
    c_r,
    rc_s,
    rc_r,
    rd_s,
    rd_r,
    kv_s,
    kv_r,
    g_s,
    g_r,
    loc,
    loco,
):
    chips = LINE * PLANE
    devs = 2 * chips
    m = lax.axis_index("cache")
    c = lax.axis_index("dp")
    i = m * 2 + c
    line, p = m // PLANE, m % PLANE
    width = hid.shape[1]
    pair = LINE // 2
    mine = c * pair
    other = (1 - c) * pair
    f32, bf16 = jnp.float32, jnp.bfloat16

    barrier = pltpu.get_barrier_semaphore()

    def greet(k, carry):
        j = (i + k) % devs
        pl.semaphore_signal(
            barrier, inc=1, device_id={"cache": j // 2, "dp": j % 2}, device_id_type=MESH
        )
        return carry

    lax.fori_loop(1, devs, greet, 0)

    own_w = pltpu.make_async_copy(wq.at[:, p], wbuf.at[0], loc.at[0])
    own_w.start()
    own_wo = []
    for zz in range(LINE):
        col = pl.multiple_of((zz * PLANE + p) * width, width)
        cp = pltpu.make_async_copy(wout.at[:, pl.ds(col, width)], wobuf.at[0, zz], loco.at[zz])
        cp.start()
        own_wo.append(cp)
        cp = pltpu.make_async_copy(
            wkv.at[:, pl.ds(col, width)], wkbuf.at[0, zz], loco.at[LINE + zz]
        )
        cp.start()
        own_wo.append(cp)
    own_c = pltpu.make_async_copy(ckv.at[m // (chips // KV)], cbuf.at[i], loc.at[1])
    own_c.start()
    own_f = hid[...].astype(f32)
    ss_in[...] = lax.dot_general(
        jnp.ones((8, width), f32),
        own_f * own_f,
        (((1,), (1,)), ((), ())),
        preferred_element_type=f32,
        precision=lax.Precision.HIGHEST,
    )
    pl.semaphore_wait(barrier, devs - 1)

    def remote(src, dst, ss, rs, chip, core):
        return pltpu.make_async_remote_copy(
            src_ref=src,
            dst_ref=dst,
            send_sem=ss,
            recv_sem=rs,
            device_id={"cache": chip, "dp": core},
            device_id_type=MESH,
        )

    def ss_copy(k):
        return remote(ss_in, srecv.at[k], s_s.at[k], s_r.at[k], (m + k) % chips, c)

    def start_ss(k, carry):
        ss_copy(k).start()
        return carry

    lax.fori_loop(1, chips, start_ss, 0)

    def line_chip(k):
        return ((line + k) % LINE) * PLANE + p

    def plane_chip(k):
        return line * PLANE + (p + k) % PLANE

    def back_chip(k):
        return line * PLANE + (p + PLANE - k) % PLANE

    inner = jnp.logical_and(line > 0, line < LINE - 1)

    def direct(k):
        if k == LINE - 1:
            return line != 0
        if k == 1:
            return line != LINE - 1
        return None

    def when(cond, act):
        if cond is None:
            act()
        else:
            pl.when(cond)(act)

    def relay(buf, ss, rs):
        slot = 2 * line - 1
        return remote(
            buf.at[2], buf.at[slot], ss.at[0], rs.at[slot], 3 * (line - 1) * PLANE + p, c
        )

    o_cp, h_cp, w_cp, wo_cp, wk_cp = {}, {}, {}, {}, {}
    def send_rows(src, buf, ss, rs, cps):
        for k in range(1, PLANE):
            for h in range(pair):
                col = pl.multiple_of(((mine + h) * PLANE + (p + k) % PLANE) * width, width)
                cps[k, h] = remote(
                    src.at[:, pl.ds(col, width)],
                    buf.at[k, mine + h],
                    ss.at[k, h],
                    rs.at[k, h],
                    plane_chip(k),
                    c,
                )
                cps[k, h].start()

    for k in (2, 1, 3):
        h_cp[k] = remote(hid, hbuf.at[k], h_s.at[k], h_r.at[k], line_chip(k), c)
        when(direct(k), h_cp[k].start)
    for k in range(1, PLANE):
        w_cp[k] = remote(
            wq.at[pl.ds(mine, pair), (p + k) % PLANE],
            wbuf.at[k, pl.ds(mine, pair)],
            w_s.at[k],
            w_r.at[k],
            plane_chip(k),
            c,
        )
        w_cp[k].start()
    send_rows(wkv, wkbuf, wk_s, wk_r, wk_cp)

    def c_copy(k):
        j = (i + k) % devs
        return remote(
            ckv.at[(j // 2) // (chips // KV)], cbuf.at[i], c_s.at[k], c_r.at[k], j // 2, j % 2
        )

    def start_c(k, carry):
        c_copy(k).start()
        return carry

    lax.fori_loop(1, devs, start_c, 0)

    for k in (2, 1, 3):
        o_cp[k] = remote(og, obuf.at[k], o_s.at[k], o_r.at[k], line_chip(k), c)
        when(direct(k), o_cp[k].start)

    send_rows(wout, wobuf, wo_s, wo_r, wo_cp)
    h_cp[2].wait_recv()

    @pl.when(inner)
    def _():
        relay(hbuf, h_s, h_r).start()

    wf_cp, wkf_cp = {}, {}
    for k in range(1, PLANE):
        w_cp[k].wait_recv()
        part = wbuf.at[k, pl.ds(mine, pair)]
        wf_cp[k] = remote(part, part, wf_s.at[k], wf_r.at[k], m, 1 - c)
        wf_cp[k].start()
        for h in range(pair):
            wk_cp[k, h].wait_recv()
            part = wkbuf.at[k, mine + h]
            wkf_cp[k, h] = remote(part, part, wkf_s.at[k, h], wkf_r.at[k, h], m, 1 - c)
            wkf_cp[k, h].start()

    unit = (
        lax.broadcasted_iota(jnp.int32, (128, 128), 0)
        == lax.broadcasted_iota(jnp.int32, (128, 128), 1)
    ).astype(f32)
    eye = unit.astype(bf16)

    def flip(table):
        return lax.dot_general(
            unit,
            table,
            (((1,), (1,)), ((), ())),
            preferred_element_type=f32,
            precision=lax.Precision.HIGHEST,
        )

    cos_t, sin_t = flip(cosd[...]), flip(sind[...])

    def wait_ss(k, carry):
        ss_copy(k).wait()
        return carry

    lax.fori_loop(1, chips, wait_ss, 0)
    srecv[0] = ss_in[...]
    total = jnp.sum(srecv[...], axis=0)
    spread = lax.dot_general(
        total,
        jnp.full((8, 128), 0.125, f32),
        (((0,), (0,)), ((), ())),
        preferred_element_type=f32,
        precision=lax.Precision.HIGHEST,
    )
    inv = lax.rsqrt(spread[:, :1] * (1.0 / (width * chips)) + 1e-05)
    own_w.wait()
    for cp in own_wo:
        cp.wait()
    for k in range(1, PLANE):
        wf_cp[k].wait_recv()
        for h in range(pair):
            wkf_cp[k, h].wait_recv()
    for kz in range(LINE):
        zz = (line + LINE - kz) % LINE
        if kz == 0:
            block = hid[...]
        else:
            if kz != 2:
                h_cp[kz].wait_recv()
            block = hbuf[kz]
        normed = (block.astype(f32) * inv * gain[zz * PLANE + p]).astype(bf16)

        def add_c(k, carry):
            term = jnp.dot(normed, wbuf[k, zz], preferred_element_type=f32)
            term_kv = lax.dot_general(
                normed, wkbuf[k, zz], (((1,), (1,)), ((), ())), preferred_element_type=f32
            )
            if kz == 0:
                cpart[k, :, :128] = term
                cpart[k, :, 128:] = term_kv
            else:
                cpart[k, :, :128] = cpart[k, :, :128] + term
                cpart[k, :, 128:] = cpart[k, :, 128:] + term_kv
            return carry

        lax.fori_loop(0, PLANE, add_c, 0)

    rc_cp = {}
    for k in range(1, PLANE):
        rc_cp[k] = remote(cpart.at[k], crecv.at[k], rc_s.at[k], rc_r.at[k], back_chip(k), c)
        rc_cp[k].start()

    o_cp[2].wait_recv()

    @pl.when(inner)
    def _():
        relay(obuf, o_s, o_r).start()

    wof_cp = {}
    for k in range(1, PLANE):
        for h in range(pair):
            wo_cp[k, h].wait_recv()
            wof_cp[k, h] = remote(
                wobuf.at[k, mine + h],
                wobuf.at[k, mine + h],
                wof_s.at[k, h],
                wof_r.at[k, h],
                m,
                1 - c,
            )
            wof_cp[k, h].start()
    qkv = cpart[0]
    for k in range(1, PLANE):
        rc_cp[k].wait_recv()
        qkv = qkv + crecv[k]
    kv = qkv[:, 128:].astype(bf16)
    kvt[...] = lax.dot_general(
        eye, kv, (((1,), (1,)), ((), ())), preferred_element_type=f32
    ).astype(bf16)

    def kv_part(chip):
        return kvt.at[pl.ds(pl.multiple_of((chip // (chips // KV)) * 16, 16), 16)]

    def kv_copy(k):
        j = (m + k) % chips
        return remote(kv_part(j), kvr.at[m], kv_s.at[k], kv_r.at[k], j, c)

    def start_kv(k, carry):
        kv_copy(k).start()
        return carry

    lax.fori_loop(1, chips, start_kv, 0)
    own_kv = pltpu.make_async_copy(kv_part(m), kvr.at[m], loc.at[2])
    own_kv.start()

    own_c.wait()

    def wait_c(k, carry):
        c_copy(k).wait()
        return carry

    lax.fori_loop(1, devs, wait_c, 0)
    rows = total_grad.shape[1]
    cache_len = rows * devs
    head_k = cbuf[:, :rows, :].reshape(cache_len, 128)
    head_v = cbuf[:, rows:, :].reshape(cache_len, 128)
    scale = 128 ** (-0.5)
    q_raw = qkv[:, :128]
    turned = jnp.concatenate([q_raw[:, 64:], q_raw[:, :64]], axis=1)
    query = (q_raw * cosd[...] + turned * sind[...]).astype(bf16)
    query_t = lax.dot_general(
        eye, query, (((1,), (1,)), ((), ())), preferred_element_type=f32
    ).astype(bf16)
    score = jnp.dot(head_k, query_t, preferred_element_type=f32) * scale
    top = jnp.max(score, axis=0, keepdims=True)

    def wait_kv(k, carry):
        kv_copy(k).wait()
        return carry

    lax.fori_loop(1, chips, wait_kv, 0)
    own_kv.wait()
    kvf = kvr[...].astype(f32)
    key_t = kvf[:, :8, :].reshape(128, kvf.shape[2])
    value_t = kvf[:, 8:, :].reshape(128, kvf.shape[2]).astype(bf16)
    turned_t = jnp.concatenate([key_t[64:], key_t[:64]], axis=0)
    key_t = (key_t * cos_t + turned_t * sin_t).astype(bf16)
    score_self = (
        lax.dot_general(key_t, query_t, (((0,), (0,)), ((), ())), preferred_element_type=f32)
        * scale
    )
    source = lax.broadcasted_iota(jnp.int32, score_self.shape, 0)
    target = lax.broadcasted_iota(jnp.int32, score_self.shape, 1)
    first, last = jnp.zeros_like(target), lengths[0, 0]
    for n in range(1, lengths.shape[1]):
        first = jnp.where(target >= last, last, first)
        last = last + lengths[0, n]
    allowed = jnp.logical_and(source <= target, source >= first)
    score_self = jnp.where(allowed, score_self, -1e30)
    top = jnp.maximum(top, jnp.max(score_self, axis=0, keepdims=True))
    e_cache = jnp.exp(score - top)
    e_self = jnp.exp(score_self - top)
    inverse = 1.0 / (
        jnp.sum(e_cache, axis=0, keepdims=True) + jnp.sum(e_self, axis=0, keepdims=True)
    )
    prob = e_cache * inverse
    weight = prob.astype(bf16)
    weight_self = (e_self * inverse).astype(bf16)
    for k in range(1, PLANE):
        for h in range(pair):
            wof_cp[k, h].wait_recv()

    for kz in range(LINE):
        if kz == 0:
            block = og[...]
        else:
            if kz != 2:
                o_cp[kz].wait_recv()
            block = obuf[kz]
        zz = (line + LINE - kz) % LINE

        def add_d(k, carry):
            term = lax.dot_general(
                block, wobuf[k, zz], (((1,), (1,)), ((), ())), preferred_element_type=f32
            )
            if kz == 0:
                dpart[k] = term
            else:
                dpart[k] = dpart[k] + term
            return carry

        lax.fori_loop(0, PLANE, add_d, 0)

    rd_cp = {}
    for k in range(1, PLANE):
        rd_cp[k] = remote(dpart.at[k], drecv.at[k], rd_s.at[k], rd_r.at[k], back_chip(k), c)
        rd_cp[k].start()

    grad = dpart[0]
    for k in range(1, PLANE):
        rd_cp[k].wait_recv()
        grad = grad + drecv[k]
    grad = grad.astype(bf16)
    grad_t = lax.dot_general(
        eye, grad, (((1,), (1,)), ((), ())), preferred_element_type=f32
    )
    grad_prob = lax.dot_general(
        head_v, grad, (((1,), (1,)), ((), ())), preferred_element_type=f32
    )

    attended = lax.dot_general(
        head_v, weight, (((0,), (0,)), ((), ())), preferred_element_type=f32
    ) + jnp.dot(value_t, weight_self, preferred_element_type=f32)
    delta = jnp.sum(grad_t * attended, axis=0, keepdims=True)
    grad_score = (prob * (grad_prob - delta)).astype(bf16)
    value_part = jnp.dot(weight, grad, preferred_element_type=f32).astype(bf16)
    key_part = (jnp.dot(grad_score, query, preferred_element_type=f32) * scale).astype(bf16)
    gsend[:, :rows, :] = key_part.reshape(devs, rows, 128)
    gsend[:, rows:, :] = value_part.reshape(devs, rows, 128)

    def g_copy(k):
        j = (i + k) % devs
        return remote(gsend.at[j], grecv.at[i], g_s.at[k], g_r.at[k], j // 2, j % 2)

    def start_g(k, carry):
        g_copy(k).start()
        return carry

    lax.fori_loop(1, devs, start_g, 0)
    own_g = pltpu.make_async_copy(gsend.at[i], grecv.at[i], loc.at[3])
    own_g.start()

    for k in range(1, LINE):
        when(direct(k), o_cp[k].wait_send)
        when(direct(k), h_cp[k].wait_send)

    @pl.when(inner)
    def _():
        relay(obuf, o_s, o_r).wait_send()
        relay(hbuf, h_s, h_r).wait_send()

    for k in range(1, PLANE):
        w_cp[k].wait_send()
        wf_cp[k].wait_send()
        rd_cp[k].wait_send()
        rc_cp[k].wait_send()
        for h in range(pair):
            wo_cp[k, h].wait_send()
            wof_cp[k, h].wait_send()
            wk_cp[k, h].wait_send()
            wkf_cp[k, h].wait_send()

    def wait_g(k, carry):
        g_copy(k).wait()
        return carry

    lax.fori_loop(1, devs, wait_g, 0)
    own_g.wait()

    share = devs // KV
    for g in range(KV):
        got = jnp.sum(grecv[g * share : (g + 1) * share].astype(f32), axis=0)
        cols = slice(g * 128, (g + 1) * 128)
        for which in range(2):
            total_grad[which, :, cols] = got[which * rows : (which + 1) * rows]


def fused_device(
    hidden,
    out_grad,
    norm_gain,
    w_query,
    w_key,
    w_value,
    w_out,
    cache_keys,
    cache_values,
    first_moment,
    second_moment,
    conv_lengths,
    row_offsets,
):
    chips = LINE * PLANE
    devs = 2 * chips
    f32, bf16 = jnp.float32, jnp.bfloat16
    rows, width = hidden.shape
    pos = cache_keys.shape[0]
    cache_len = pos * devs
    head = w_query.shape[1]
    full = w_query.shape[0]
    w_kv = jnp.stack([w_key.transpose(1, 2, 0), w_value.transpose(1, 2, 0)], axis=1)
    w_kv = w_kv.reshape(head, full)
    ckv = jnp.stack(
        [cache_keys.astype(bf16).reshape(pos, KV, head), cache_values.astype(bf16).reshape(pos, KV, head)]
    )
    ckv = ckv.transpose(2, 0, 1, 3).reshape(KV, 2 * pos, head)
    segment, position = row_layout(conv_lengths[0], row_offsets[0], rows, cache_len)
    cos, sin = rope_tables(position, head)
    cosd = jnp.concatenate([cos, cos], axis=1)
    sind = jnp.concatenate([-sin, sin], axis=1)
    vm = pl.BlockSpec(memory_space=pltpu.VMEM)
    smem = pl.BlockSpec(memory_space=pltpu.SMEM)
    hbm = pl.BlockSpec(memory_space=pl.ANY)
    dma = pltpu.SemaphoreType.DMA
    pair = LINE // 2
    gradient = pl.pallas_call(
        fused_kernel,
        out_shape=jax.ShapeDtypeStruct(first_moment.shape, f32),
        in_specs=[vm, vm, vm, hbm, hbm, hbm, vm, vm, vm, smem],
        out_specs=vm,
        scratch_shapes=[
            pltpu.VMEM((LINE, rows, width), bf16),
            pltpu.VMEM((LINE, rows, width), bf16),
            pltpu.VMEM((8, rows), f32),
            pltpu.VMEM((chips, 8, rows), f32),
            pltpu.VMEM((PLANE, LINE, width, head), bf16),
            pltpu.VMEM((PLANE, LINE, head, width), bf16),
            pltpu.VMEM((PLANE, LINE, head, width), bf16),
            pltpu.VMEM((devs, 2 * pos, head), bf16),
            pltpu.VMEM((PLANE, rows, 2 * head), f32),
            pltpu.VMEM((PLANE, rows, 2 * head), f32),
            pltpu.VMEM((PLANE, rows, head), f32),
            pltpu.VMEM((PLANE, rows, head), f32),
            pltpu.VMEM((head, rows), bf16),
            pltpu.VMEM((chips, 16, rows), bf16),
            pltpu.VMEM((devs, 2 * pos, head), bf16),
            pltpu.VMEM((devs, 2 * pos, head), bf16),
            dma((LINE,)),
            dma((LINE,)),
            dma((LINE,)),
            dma((LINE,)),
            dma((chips,)),
            dma((chips,)),
            dma((PLANE,)),
            dma((PLANE,)),
            dma((PLANE,)),
            dma((PLANE,)),
            dma((PLANE, pair)),
            dma((PLANE, pair)),
            dma((PLANE, pair)),
            dma((PLANE, pair)),
            dma((PLANE, pair)),
            dma((PLANE, pair)),
            dma((PLANE, pair)),
            dma((PLANE, pair)),
            dma((devs,)),
            dma((devs,)),
            dma((PLANE,)),
            dma((PLANE,)),
            dma((PLANE,)),
            dma((PLANE,)),
            dma((chips,)),
            dma((chips,)),
            dma((devs,)),
            dma((devs,)),
            dma((4,)),
            dma((2 * LINE,)),
        ],
        compiler_params=pltpu.CompilerParams(
            collective_id=0, has_side_effects=True, vmem_limit_bytes=56 * 1024 * 1024
        ),
    )(
        hidden,
        out_grad,
        norm_gain.reshape(chips, 1, width),
        w_query.reshape(LINE, PLANE, width, head),
        w_kv,
        w_out,
        ckv,
        cosd,
        sind,
        conv_lengths,
    )
    new_keys, first_k, second_k = adam_update(
        cache_keys, gradient[0], first_moment[0], second_moment[0]
    )
    new_values, first_v, second_v = adam_update(
        cache_values, gradient[1], first_moment[1], second_moment[1]
    )
    return (new_keys, new_values, jnp.stack([first_k, first_v]), jnp.stack([second_k, second_v]))


def solution(mesh):
    return jax.shard_map(
        fused_device if fits(mesh) else per_device,
        mesh=mesh,
        in_specs=(
            P(("groups", "dp"), "cache"),
            P(("groups", "dp"), "cache"),
            P(),
            P(None, "cache"),
            P(None, None, "cache"),
            P(None, None, "cache"),
            P("cache", None),
            P(("groups", "cache", "dp"), None),
            P(("groups", "cache", "dp"), None),
            P(None, ("groups", "cache", "dp"), None),
            P(None, ("groups", "cache", "dp"), None),
            P(("groups", "dp"), None),
            P(("groups", "dp"), None),
        ),
        out_specs=(
            P(("groups", "cache", "dp"), None),
            P(("groups", "cache", "dp"), None),
            P(None, ("groups", "cache", "dp"), None),
            P(None, ("groups", "cache", "dp"), None),
        ),
        check_vma=False,
    )
```

```python
import math

import jax
import jax.numpy as jnp
from jax import lax
from jax.experimental import pallas as pl
from jax.experimental.pallas import tpu as pltpu
from jax.sharding import PartitionSpec as P

KV = 8
ADAM_STEP = 10


THETA = 500000.0
BETA_ONE = 0.9
BETA_TWO = 0.999
RATE = 0.02
EPSILON = 1e-08


def rope_tables(position, head_width):
    half_width = head_width // 2
    inverse = jnp.exp(
        jnp.arange(half_width, dtype=jnp.float32) * (-2.0 * math.log(THETA) / head_width)
    )
    angles = position.astype(jnp.float32)[:, None] * inverse[None, :]
    return (jnp.cos(angles), jnp.sin(angles))


def rotate(tensor, cos_table, sin_table):
    half_width = tensor.shape[1] // 2
    first_half = tensor[:, :half_width]
    second_half = tensor[:, half_width:]
    return jnp.concatenate(
        [
            first_half * cos_table - second_half * sin_table,
            second_half * cos_table + first_half * sin_table,
        ],
        axis=1,
    )


def row_layout(lengths, offsets, row_count, cache_len):
    end_rows = jnp.cumsum(lengths)
    start_rows = end_rows - lengths
    row_index = jnp.arange(row_count, dtype=jnp.int32)
    segment = jnp.sum((row_index[:, None] >= end_rows[None, :]).astype(jnp.int32), axis=1)
    onehot = segment[:, None] == jnp.arange(lengths.shape[0], dtype=jnp.int32)[None, :]
    first_row = jnp.sum(jnp.where(onehot, start_rows[None, :], 0), axis=1)
    offset_row = jnp.sum(jnp.where(onehot, offsets[None, :], 0), axis=1)
    return (segment, cache_len + offset_row + row_index - first_row)


def attend(query, grad_out, cache_k, cache_v, self_k, self_v, allowed, score_scale):
    contract = (((1,), (1,)), ((), ()))
    score_cache = (
        lax.dot_general(query, cache_k, contract, preferred_element_type=jnp.float32) * score_scale
    )
    score_self = (
        lax.dot_general(query, self_k, contract, preferred_element_type=jnp.float32) * score_scale
    )
    score_self = jnp.where(allowed, score_self, -1e30)
    highest = jnp.maximum(
        jnp.max(score_cache, axis=1, keepdims=True), jnp.max(score_self, axis=1, keepdims=True)
    )
    exp_cache = jnp.exp(score_cache - highest)
    exp_self = jnp.exp(score_self - highest)
    denominator = jnp.sum(exp_cache, axis=1, keepdims=True) + jnp.sum(
        exp_self, axis=1, keepdims=True
    )
    prob_cache = exp_cache / denominator
    prob_self = exp_self / denominator
    weight_cache = prob_cache.astype(jnp.bfloat16)
    weight_self = prob_self.astype(jnp.bfloat16)
    attended = jnp.dot(weight_cache, cache_v, preferred_element_type=jnp.float32) + jnp.dot(
        weight_self, self_v, preferred_element_type=jnp.float32
    )
    delta_row = jnp.sum(grad_out.astype(jnp.float32) * attended, axis=1, keepdims=True)
    grad_prob = lax.dot_general(grad_out, cache_v, contract, preferred_element_type=jnp.float32)
    grad_score = (prob_cache * (grad_prob - delta_row)).astype(jnp.bfloat16)
    return (grad_score, weight_cache)


def adam_update(master, gradient, first, second):
    first_new = BETA_ONE * first + (1.0 - BETA_ONE) * gradient
    second_new = BETA_TWO * second + (1.0 - BETA_TWO) * gradient * gradient
    first_hat = first_new / (1.0 - BETA_ONE**ADAM_STEP)
    second_hat = second_new / (1.0 - BETA_TWO**ADAM_STEP)
    return (master - RATE * first_hat / (jnp.sqrt(second_hat) + EPSILON), first_new, second_new)


def source_total(pieces):
    head_width = pieces.shape[2]
    item_count = pieces.shape[1]
    summed = (
        pieces.astype(jnp.float32)
        .reshape(KV, pieces.shape[0] // KV, item_count, head_width)
        .sum(axis=1)
    )
    return summed.transpose(1, 0, 2).reshape(item_count, KV * head_width)


def totals_pair(pieces):
    return (source_total(pieces[0]), source_total(pieces[1]))


def per_device(
    hidden,
    out_grad,
    norm_gain,
    w_query,
    w_key,
    w_value,
    w_out,
    cache_keys,
    cache_values,
    first_moment,
    second_moment,
    conv_lengths,
    row_offsets,
):
    cache_count = lax.axis_size("cache")
    data_count = lax.axis_size("dp")
    pos_count = cache_keys.shape[0]
    device_count = cache_count * data_count
    cache_len = pos_count * device_count
    head_width = w_query.shape[1]
    column_share = w_key.shape[2]
    groups = cache_count // KV
    kv_head = lax.axis_index("cache") // groups
    score_scale = head_width ** (-0.5)
    hidden_full, grad_full = (
        lax.all_gather(hidden, "cache", axis=1, tiled=True),
        lax.all_gather(out_grad, "cache", axis=1, tiled=True),
    )
    row_count = hidden_full.shape[0]
    width_full = hidden_full.shape[1]
    hidden_f = hidden_full.astype(jnp.float32)
    inv_rms = lax.rsqrt(jnp.mean(hidden_f * hidden_f, axis=1, keepdims=True) + 1e-05)
    normed = (hidden_f * inv_rms * norm_gain).astype(jnp.bfloat16)
    segment, position = row_layout(conv_lengths[0], row_offsets[0], row_count, cache_len)
    cos_table, sin_table = rope_tables(position, head_width)
    query = rotate(
        jnp.dot(normed, w_query, preferred_element_type=jnp.float32), cos_table, sin_table
    ).astype(jnp.bfloat16)
    key_piece = (
        jnp.dot(
            normed, w_key.reshape(width_full, KV * column_share), preferred_element_type=jnp.float32
        )
        .astype(jnp.bfloat16)
        .reshape(row_count, KV, column_share)
    )
    value_piece = (
        jnp.dot(
            normed,
            w_value.reshape(width_full, KV * column_share),
            preferred_element_type=jnp.float32,
        )
        .astype(jnp.bfloat16)
        .reshape(row_count, KV, column_share)
    )
    keys_raw, values_self = (
        lax.all_gather(key_piece, "cache", axis=2, tiled=True),
        lax.all_gather(value_piece, "cache", axis=2, tiled=True),
    )
    own_keys = lax.dynamic_slice_in_dim(keys_raw, kv_head, 1, 1).reshape(row_count, head_width)
    self_k = rotate(own_keys.astype(jnp.float32), cos_table, sin_table).astype(jnp.bfloat16)
    self_v = lax.dynamic_slice_in_dim(values_self, kv_head, 1, 1).reshape(row_count, head_width)
    grad_out = lax.dot_general(
        grad_full, w_out, (((1,), (1,)), ((), ())), preferred_element_type=jnp.float32
    ).astype(jnp.bfloat16)
    cache_k = cache_keys.astype(jnp.bfloat16)
    cache_v = cache_values.astype(jnp.bfloat16)
    keys_all, values_all = (
        lax.all_gather(cache_k, ("cache", "dp"), axis=0, tiled=True),
        lax.all_gather(cache_v, ("cache", "dp"), axis=0, tiled=True),
    )
    head_k = lax.dynamic_slice_in_dim(keys_all, kv_head * head_width, head_width, 1)
    head_v = lax.dynamic_slice_in_dim(values_all, kv_head * head_width, head_width, 1)
    row_index = jnp.arange(row_count, dtype=jnp.int32)
    allowed = (segment[:, None] == segment[None, :]) & (row_index[None, :] <= row_index[:, None])
    grad_score, weight_cache = attend(
        query, grad_out, head_k, head_v, self_k, self_v, allowed, score_scale
    )
    transposed = (((0,), (0,)), ((), ()))
    key_part = (
        lax.dot_general(grad_score, query, transposed, preferred_element_type=jnp.float32)
        * score_scale
    ).astype(jnp.bfloat16)
    value_part = lax.dot_general(
        weight_cache, grad_out, transposed, preferred_element_type=jnp.float32
    ).astype(jnp.bfloat16)
    send_k = key_part.reshape(device_count, pos_count, head_width)
    send_v = value_part.reshape(device_count, pos_count, head_width)
    grad_k, grad_v = totals_pair(
        (
            lax.all_to_all(send_k, ("cache", "dp"), split_axis=0, concat_axis=0, tiled=True),
            lax.all_to_all(send_v, ("cache", "dp"), split_axis=0, concat_axis=0, tiled=True),
        )
    )
    gradient = jnp.stack([grad_k, grad_v])
    master = jnp.stack([cache_keys, cache_values])
    new_master, first_new, second_new = adam_update(master, gradient, first_moment, second_moment)
    return (new_master[0], new_master[1], first_new, second_new)


LINE = 4
PLANE = 4
MESH = pl.DeviceIdType.MESH


def fits(mesh):
    return mesh.shape["cache"] == LINE * PLANE and mesh.shape["dp"] == 2


def fused_kernel(
    hid,
    og,
    gain,
    wq,
    wkv,
    wout,
    ckv,
    cosd,
    sind,
    lengths,
    total_grad,
    hbuf,
    obuf,
    ss_in,
    srecv,
    wbuf,
    wkbuf,
    wobuf,
    cbuf,
    cpart,
    crecv,
    dpart,
    drecv,
    kvt,
    kvr,
    gsend,
    grecv,
    h_s,
    h_r,
    o_s,
    o_r,
    s_s,
    s_r,
    w_s,
    w_r,
    wf_s,
    wf_r,
    wk_s,
    wk_r,
    wkf_s,
    wkf_r,
    wo_s,
    wo_r,
    wof_s,
    wof_r,
    c_s,
    c_r,
    rc_s,
    rc_r,
    rd_s,
    rd_r,
    kv_s,
    kv_r,
    g_s,
    g_r,
    loc,
    loco,
):
    chips = LINE * PLANE
    devs = 2 * chips
    m = lax.axis_index("cache")
    c = lax.axis_index("dp")
    i = m * 2 + c
    line, p = m // PLANE, m % PLANE
    width = hid.shape[1]
    pair = LINE // 2
    mine = c * pair
    other = (1 - c) * pair
    f32, bf16 = jnp.float32, jnp.bfloat16

    barrier = pltpu.get_barrier_semaphore()

    def greet(k, carry):
        j = (i + k) % devs
        pl.semaphore_signal(
            barrier, inc=1, device_id={"cache": j // 2, "dp": j % 2}, device_id_type=MESH
        )
        return carry

    lax.fori_loop(1, devs, greet, 0)

    own_w = pltpu.make_async_copy(wq.at[:, p], wbuf.at[0], loc.at[0])
    own_w.start()
    own_wo = []
    for zz in range(LINE):
        col = pl.multiple_of((zz * PLANE + p) * width, width)
        cp = pltpu.make_async_copy(wout.at[:, pl.ds(col, width)], wobuf.at[0, zz], loco.at[zz])
        cp.start()
        own_wo.append(cp)
        cp = pltpu.make_async_copy(
            wkv.at[:, pl.ds(col, width)], wkbuf.at[0, zz], loco.at[LINE + zz]
        )
        cp.start()
        own_wo.append(cp)
    own_c = pltpu.make_async_copy(ckv.at[m // (chips // KV)], cbuf.at[i], loc.at[1])
    own_c.start()
    own_f = hid[...].astype(f32)
    ss_in[...] = lax.dot_general(
        jnp.ones((8, width), f32),
        own_f * own_f,
        (((1,), (1,)), ((), ())),
        preferred_element_type=f32,
        precision=lax.Precision.HIGHEST,
    )
    pl.semaphore_wait(barrier, devs - 1)

    def remote(src, dst, ss, rs, chip, core):
        return pltpu.make_async_remote_copy(
            src_ref=src,
            dst_ref=dst,
            send_sem=ss,
            recv_sem=rs,
            device_id={"cache": chip, "dp": core},
            device_id_type=MESH,
        )

    def ss_copy(k):
        return remote(ss_in, srecv.at[k], s_s.at[k], s_r.at[k], (m + k) % chips, c)

    def start_ss(k, carry):
        ss_copy(k).start()
        return carry

    lax.fori_loop(1, chips, start_ss, 0)

    def line_chip(k):
        return ((line + k) % LINE) * PLANE + p

    def plane_chip(k):
        return line * PLANE + (p + k) % PLANE

    def back_chip(k):
        return line * PLANE + (p + PLANE - k) % PLANE

    inner = jnp.logical_and(line > 0, line < LINE - 1)

    def direct(k):
        if k == LINE - 1:
            return line != 0
        if k == 1:
            return line != LINE - 1
        return None

    def when(cond, act):
        if cond is None:
            act()
        else:
            pl.when(cond)(act)

    def relay(buf, ss, rs):
        slot = 2 * line - 1
        return remote(
            buf.at[2], buf.at[slot], ss.at[0], rs.at[slot], 3 * (line - 1) * PLANE + p, c
        )

    o_cp, h_cp, w_cp, wo_cp, wk_cp = {}, {}, {}, {}, {}
    def send_rows(src, buf, ss, rs, cps):
        for k in range(1, PLANE):
            for h in range(pair):
                col = pl.multiple_of(((mine + h) * PLANE + (p + k) % PLANE) * width, width)
                cps[k, h] = remote(
                    src.at[:, pl.ds(col, width)],
                    buf.at[k, mine + h],
                    ss.at[k, h],
                    rs.at[k, h],
                    plane_chip(k),
                    c,
                )
                cps[k, h].start()

    for k in (2, 1, 3):
        h_cp[k] = remote(hid, hbuf.at[k], h_s.at[k], h_r.at[k], line_chip(k), c)
        when(direct(k), h_cp[k].start)
    for k in range(1, PLANE):
        w_cp[k] = remote(
            wq.at[pl.ds(mine, pair), (p + k) % PLANE],
            wbuf.at[k, pl.ds(mine, pair)],
            w_s.at[k],
            w_r.at[k],
            plane_chip(k),
            c,
        )
        w_cp[k].start()
    send_rows(wkv, wkbuf, wk_s, wk_r, wk_cp)

    def c_copy(k):
        j = (i + k) % devs
        return remote(
            ckv.at[(j // 2) // (chips // KV)], cbuf.at[i], c_s.at[k], c_r.at[k], j // 2, j % 2
        )

    def start_c(k, carry):
        c_copy(k).start()
        return carry

    lax.fori_loop(1, devs, start_c, 0)

    h_cp[2].wait_recv()

    @pl.when(inner)
    def _():
        relay(hbuf, h_s, h_r).start()

    wf_cp, wkf_cp = {}, {}
    for k in range(1, PLANE):
        w_cp[k].wait_recv()
        part = wbuf.at[k, pl.ds(mine, pair)]
        wf_cp[k] = remote(part, part, wf_s.at[k], wf_r.at[k], m, 1 - c)
        wf_cp[k].start()
        for h in range(pair):
            wk_cp[k, h].wait_recv()
            part = wkbuf.at[k, mine + h]
            wkf_cp[k, h] = remote(part, part, wkf_s.at[k, h], wkf_r.at[k, h], m, 1 - c)
            wkf_cp[k, h].start()

    for k in (2, 1, 3):
        o_cp[k] = remote(og, obuf.at[k], o_s.at[k], o_r.at[k], line_chip(k), c)
        when(direct(k), o_cp[k].start)

    send_rows(wout, wobuf, wo_s, wo_r, wo_cp)
    unit = (
        lax.broadcasted_iota(jnp.int32, (128, 128), 0)
        == lax.broadcasted_iota(jnp.int32, (128, 128), 1)
    ).astype(f32)
    eye = unit.astype(bf16)

    def flip(table):
        return lax.dot_general(
            unit,
            table,
            (((1,), (1,)), ((), ())),
            preferred_element_type=f32,
            precision=lax.Precision.HIGHEST,
        )

    cos_t, sin_t = flip(cosd[...]), flip(sind[...])

    def wait_ss(k, carry):
        ss_copy(k).wait()
        return carry

    lax.fori_loop(1, chips, wait_ss, 0)
    srecv[0] = ss_in[...]
    total = jnp.sum(srecv[...], axis=0)
    spread = lax.dot_general(
        total,
        jnp.full((8, 128), 0.125, f32),
        (((0,), (0,)), ((), ())),
        preferred_element_type=f32,
        precision=lax.Precision.HIGHEST,
    )
    inv = lax.rsqrt(spread[:, :1] * (1.0 / (width * chips)) + 1e-05)
    own_w.wait()
    for cp in own_wo:
        cp.wait()
    for k in range(1, PLANE):
        wf_cp[k].wait_recv()
        for h in range(pair):
            wkf_cp[k, h].wait_recv()
    for kz in range(LINE):
        zz = (line + LINE - kz) % LINE
        if kz == 0:
            block = hid[...]
        else:
            if kz != 2:
                h_cp[kz].wait_recv()
            block = hbuf[kz]
        normed = (block.astype(f32) * inv * gain[zz * PLANE + p]).astype(bf16)

        def add_c(k, carry):
            term = jnp.dot(normed, wbuf[k, zz], preferred_element_type=f32)
            term_kv = lax.dot_general(
                normed, wkbuf[k, zz], (((1,), (1,)), ((), ())), preferred_element_type=f32
            )
            if kz == 0:
                cpart[k, :, :128] = term
                cpart[k, :, 128:] = term_kv
            else:
                cpart[k, :, :128] = cpart[k, :, :128] + term
                cpart[k, :, 128:] = cpart[k, :, 128:] + term_kv
            return carry

        lax.fori_loop(0, PLANE, add_c, 0)

    rc_cp = {}
    for k in range(1, PLANE):
        rc_cp[k] = remote(cpart.at[k], crecv.at[k], rc_s.at[k], rc_r.at[k], back_chip(k), c)
        rc_cp[k].start()

    o_cp[2].wait_recv()

    @pl.when(inner)
    def _():
        relay(obuf, o_s, o_r).start()

    wof_cp = {}
    for k in range(1, PLANE):
        for h in range(pair):
            wo_cp[k, h].wait_recv()
            wof_cp[k, h] = remote(
                wobuf.at[k, mine + h],
                wobuf.at[k, mine + h],
                wof_s.at[k, h],
                wof_r.at[k, h],
                m,
                1 - c,
            )
            wof_cp[k, h].start()
    qkv = cpart[0]
    for k in range(1, PLANE):
        rc_cp[k].wait_recv()
        qkv = qkv + crecv[k]
    kv = qkv[:, 128:].astype(bf16)
    kvt[...] = lax.dot_general(
        eye, kv, (((1,), (1,)), ((), ())), preferred_element_type=f32
    ).astype(bf16)

    def kv_part(chip):
        return kvt.at[pl.ds(pl.multiple_of((chip // (chips // KV)) * 16, 16), 16)]

    def kv_copy(k):
        j = (m + k) % chips
        return remote(kv_part(j), kvr.at[m], kv_s.at[k], kv_r.at[k], j, c)

    def start_kv(k, carry):
        kv_copy(k).start()
        return carry

    lax.fori_loop(1, chips, start_kv, 0)
    own_kv = pltpu.make_async_copy(kv_part(m), kvr.at[m], loc.at[2])
    own_kv.start()

    own_c.wait()

    def wait_c(k, carry):
        c_copy(k).wait()
        return carry

    lax.fori_loop(1, devs, wait_c, 0)
    rows = total_grad.shape[1]
    cache_len = rows * devs
    head_k = cbuf[:, :rows, :].reshape(cache_len, 128)
    head_v = cbuf[:, rows:, :].reshape(cache_len, 128)
    scale = 128 ** (-0.5)
    q_raw = qkv[:, :128]
    turned = jnp.concatenate([q_raw[:, 64:], q_raw[:, :64]], axis=1)
    query = (q_raw * cosd[...] + turned * sind[...]).astype(bf16)
    query_t = lax.dot_general(
        eye, query, (((1,), (1,)), ((), ())), preferred_element_type=f32
    ).astype(bf16)
    score = jnp.dot(head_k, query_t, preferred_element_type=f32) * scale
    top = jnp.max(score, axis=0, keepdims=True)

    def wait_kv(k, carry):
        kv_copy(k).wait()
        return carry

    lax.fori_loop(1, chips, wait_kv, 0)
    own_kv.wait()
    kvf = kvr[...].astype(f32)
    key_t = kvf[:, :8, :].reshape(128, kvf.shape[2])
    value_t = kvf[:, 8:, :].reshape(128, kvf.shape[2]).astype(bf16)
    turned_t = jnp.concatenate([key_t[64:], key_t[:64]], axis=0)
    key_t = (key_t * cos_t + turned_t * sin_t).astype(bf16)
    score_self = (
        lax.dot_general(key_t, query_t, (((0,), (0,)), ((), ())), preferred_element_type=f32)
        * scale
    )
    source = lax.broadcasted_iota(jnp.int32, score_self.shape, 0)
    target = lax.broadcasted_iota(jnp.int32, score_self.shape, 1)
    first, last = jnp.zeros_like(target), lengths[0, 0]
    for n in range(1, lengths.shape[1]):
        first = jnp.where(target >= last, last, first)
        last = last + lengths[0, n]
    allowed = jnp.logical_and(source <= target, source >= first)
    score_self = jnp.where(allowed, score_self, -1e30)
    top = jnp.maximum(top, jnp.max(score_self, axis=0, keepdims=True))
    e_cache = jnp.exp(score - top)
    e_self = jnp.exp(score_self - top)
    inverse = 1.0 / (
        jnp.sum(e_cache, axis=0, keepdims=True) + jnp.sum(e_self, axis=0, keepdims=True)
    )
    prob = e_cache * inverse
    weight = prob.astype(bf16)
    weight_self = (e_self * inverse).astype(bf16)
    for k in range(1, PLANE):
        for h in range(pair):
            wof_cp[k, h].wait_recv()

    for kz in range(LINE):
        if kz == 0:
            block = og[...]
        else:
            if kz != 2:
                o_cp[kz].wait_recv()
            block = obuf[kz]
        zz = (line + LINE - kz) % LINE

        def add_d(k, carry):
            term = lax.dot_general(
                block, wobuf[k, zz], (((1,), (1,)), ((), ())), preferred_element_type=f32
            )
            if kz == 0:
                dpart[k] = term
            else:
                dpart[k] = dpart[k] + term
            return carry

        lax.fori_loop(0, PLANE, add_d, 0)

    rd_cp = {}
    for k in range(1, PLANE):
        rd_cp[k] = remote(dpart.at[k], drecv.at[k], rd_s.at[k], rd_r.at[k], back_chip(k), c)
        rd_cp[k].start()

    grad = dpart[0]
    for k in range(1, PLANE):
        rd_cp[k].wait_recv()
        grad = grad + drecv[k]
    grad = grad.astype(bf16)
    grad_t = lax.dot_general(
        eye, grad, (((1,), (1,)), ((), ())), preferred_element_type=f32
    )
    grad_prob = lax.dot_general(
        head_v, grad, (((1,), (1,)), ((), ())), preferred_element_type=f32
    )

    attended = lax.dot_general(
        head_v, weight, (((0,), (0,)), ((), ())), preferred_element_type=f32
    ) + jnp.dot(value_t, weight_self, preferred_element_type=f32)
    delta = jnp.sum(grad_t * attended, axis=0, keepdims=True)
    grad_score = (prob * (grad_prob - delta)).astype(bf16)
    value_part = jnp.dot(weight, grad, preferred_element_type=f32).astype(bf16)
    key_part = (jnp.dot(grad_score, query, preferred_element_type=f32) * scale).astype(bf16)
    gsend[:, :rows, :] = key_part.reshape(devs, rows, 128)
    gsend[:, rows:, :] = value_part.reshape(devs, rows, 128)

    def g_copy(k):
        j = (i + k) % devs
        return remote(gsend.at[j], grecv.at[i], g_s.at[k], g_r.at[k], j // 2, j % 2)

    def start_g(k, carry):
        g_copy(k).start()
        return carry

    lax.fori_loop(1, devs, start_g, 0)
    own_g = pltpu.make_async_copy(gsend.at[i], grecv.at[i], loc.at[3])
    own_g.start()

    for k in range(1, LINE):
        when(direct(k), o_cp[k].wait_send)
        when(direct(k), h_cp[k].wait_send)

    @pl.when(inner)
    def _():
        relay(obuf, o_s, o_r).wait_send()
        relay(hbuf, h_s, h_r).wait_send()

    for k in range(1, PLANE):
        w_cp[k].wait_send()
        wf_cp[k].wait_send()
        rd_cp[k].wait_send()
        rc_cp[k].wait_send()
        for h in range(pair):
            wo_cp[k, h].wait_send()
            wof_cp[k, h].wait_send()
            wk_cp[k, h].wait_send()
            wkf_cp[k, h].wait_send()

    def wait_g(k, carry):
        g_copy(k).wait()
        return carry

    lax.fori_loop(1, devs, wait_g, 0)
    own_g.wait()

    share = devs // KV
    for g in range(KV):
        got = jnp.sum(grecv[g * share : (g + 1) * share].astype(f32), axis=0)
        cols = slice(g * 128, (g + 1) * 128)
        for which in range(2):
            total_grad[which, :, cols] = got[which * rows : (which + 1) * rows]


def fused_device(
    hidden,
    out_grad,
    norm_gain,
    w_query,
    w_key,
    w_value,
    w_out,
    cache_keys,
    cache_values,
    first_moment,
    second_moment,
    conv_lengths,
    row_offsets,
):
    chips = LINE * PLANE
    devs = 2 * chips
    f32, bf16 = jnp.float32, jnp.bfloat16
    rows, width = hidden.shape
    pos = cache_keys.shape[0]
    cache_len = pos * devs
    head = w_query.shape[1]
    full = w_query.shape[0]
    w_kv = jnp.stack([w_key.transpose(1, 2, 0), w_value.transpose(1, 2, 0)], axis=1)
    w_kv = w_kv.reshape(head, full)
    ckv = jnp.stack(
        [cache_keys.astype(bf16).reshape(pos, KV, head), cache_values.astype(bf16).reshape(pos, KV, head)]
    )
    ckv = ckv.transpose(2, 0, 1, 3).reshape(KV, 2 * pos, head)
    segment, position = row_layout(conv_lengths[0], row_offsets[0], rows, cache_len)
    cos, sin = rope_tables(position, head)
    cosd = jnp.concatenate([cos, cos], axis=1)
    sind = jnp.concatenate([-sin, sin], axis=1)
    vm = pl.BlockSpec(memory_space=pltpu.VMEM)
    smem = pl.BlockSpec(memory_space=pltpu.SMEM)
    hbm = pl.BlockSpec(memory_space=pl.ANY)
    dma = pltpu.SemaphoreType.DMA
    pair = LINE // 2
    gradient = pl.pallas_call(
        fused_kernel,
        out_shape=jax.ShapeDtypeStruct(first_moment.shape, f32),
        in_specs=[vm, vm, vm, hbm, hbm, hbm, vm, vm, vm, smem],
        out_specs=vm,
        scratch_shapes=[
            pltpu.VMEM((LINE, rows, width), bf16),
            pltpu.VMEM((LINE, rows, width), bf16),
            pltpu.VMEM((8, rows), f32),
            pltpu.VMEM((chips, 8, rows), f32),
            pltpu.VMEM((PLANE, LINE, width, head), bf16),
            pltpu.VMEM((PLANE, LINE, head, width), bf16),
            pltpu.VMEM((PLANE, LINE, head, width), bf16),
            pltpu.VMEM((devs, 2 * pos, head), bf16),
            pltpu.VMEM((PLANE, rows, 2 * head), f32),
            pltpu.VMEM((PLANE, rows, 2 * head), f32),
            pltpu.VMEM((PLANE, rows, head), f32),
            pltpu.VMEM((PLANE, rows, head), f32),
            pltpu.VMEM((head, rows), bf16),
            pltpu.VMEM((chips, 16, rows), bf16),
            pltpu.VMEM((devs, 2 * pos, head), bf16),
            pltpu.VMEM((devs, 2 * pos, head), bf16),
            dma((LINE,)),
            dma((LINE,)),
            dma((LINE,)),
            dma((LINE,)),
            dma((chips,)),
            dma((chips,)),
            dma((PLANE,)),
            dma((PLANE,)),
            dma((PLANE,)),
            dma((PLANE,)),
            dma((PLANE, pair)),
            dma((PLANE, pair)),
            dma((PLANE, pair)),
            dma((PLANE, pair)),
            dma((PLANE, pair)),
            dma((PLANE, pair)),
            dma((PLANE, pair)),
            dma((PLANE, pair)),
            dma((devs,)),
            dma((devs,)),
            dma((PLANE,)),
            dma((PLANE,)),
            dma((PLANE,)),
            dma((PLANE,)),
            dma((chips,)),
            dma((chips,)),
            dma((devs,)),
            dma((devs,)),
            dma((4,)),
            dma((2 * LINE,)),
        ],
        compiler_params=pltpu.CompilerParams(
            collective_id=0, has_side_effects=True, vmem_limit_bytes=56 * 1024 * 1024
        ),
    )(
        hidden,
        out_grad,
        norm_gain.reshape(chips, 1, width),
        w_query.reshape(LINE, PLANE, width, head),
        w_kv,
        w_out,
        ckv,
        cosd,
        sind,
        conv_lengths,
    )
    new_keys, first_k, second_k = adam_update(
        cache_keys, gradient[0], first_moment[0], second_moment[0]
    )
    new_values, first_v, second_v = adam_update(
        cache_values, gradient[1], first_moment[1], second_moment[1]
    )
    return (new_keys, new_values, jnp.stack([first_k, first_v]), jnp.stack([second_k, second_v]))


def solution(mesh):
    return jax.shard_map(
        fused_device if fits(mesh) else per_device,
        mesh=mesh,
        in_specs=(
            P(("groups", "dp"), "cache"),
            P(("groups", "dp"), "cache"),
            P(),
            P(None, "cache"),
            P(None, None, "cache"),
            P(None, None, "cache"),
            P("cache", None),
            P(("groups", "cache", "dp"), None),
            P(("groups", "cache", "dp"), None),
            P(None, ("groups", "cache", "dp"), None),
            P(None, ("groups", "cache", "dp"), None),
            P(("groups", "dp"), None),
            P(("groups", "dp"), None),
        ),
        out_specs=(
            P(("groups", "cache", "dp"), None),
            P(("groups", "cache", "dp"), None),
            P(None, ("groups", "cache", "dp"), None),
            P(None, ("groups", "cache", "dp"), None),
        ),
        check_vma=False,
    )
```
